512 devices in a mesh: side: 2 (over z_hi), seq: 32 (over z_lo, x, core), tp: 8 (over y).
Axes of the slice: x: 4, y: 8, z: 8 (z_hi: 2, z_lo: 4; z = z_hi * 4 + z_lo), core: 2. Of those that a mesh axis runs over, the one named last changes fastest.
Arguments:
- self_query: bfloat16 [2, 32, 1024, 2048], P('side', 'seq', None, 'tp'), may hold values from -64 to 64
- self_key: bfloat16 [2, 32, 1024, 2048], P('side', 'seq', None, 'tp'), may hold values from -64 to 64
- self_value: bfloat16 [2, 32, 1024, 2048], P('side', 'seq', None, 'tp'), may hold values from -6 to 6
- cross_query: bfloat16 [2, 32, 1024, 2048], P('side', 'seq', None, 'tp'), may hold values from -72 to 72
- passages: bfloat16 [2, 32, 16, 128, 1024], P('side', 'seq', None, None, 'tp'), may hold values from -6 to 6
- w_key: bfloat16 [1024, 2048], P(None, 'tp'), may hold values from -0.1875 to 0.1875
- w_value: bfloat16 [1024, 2048], P(None, 'tp'), may hold values from -0.1875 to 0.1875
- block_map: int32 [2, 32, 32], replicated, may hold values from 0 to 31, each once within a row
- passage_ids: int32 [2, 32, 32], replicated, may hold values from 0 to 15
Outputs:
- mixed: bfloat16 [2, 32, 1024, 2048], P('side', 'seq', None, 'tp')
The draws below stay inside these ranges and needn't reach their ends.
Inputs may be any that keep to these rules, and one draw needn't show every extreme that they name: Each row block_map[h, d, :] names every block 0 to 31 exactly once.
All inputs are finite; a program needn't handle non-finite values.
Results may differ from the reference program's by a relative error of at most 0.0069.
Values may be sent and summed in bfloat16 or wider, within the bound.
No kernel may reach another device: no remote copies, remote signals or barrier semaphores. Data moves between devices by JAX's collectives and lax.ppermute only.
A program may use at most 64 MiB of HBM per device.

```python
import math
import jax
import jax.numpy as jnp
from jax import lax

HEADS = 16
HD = 128
DE = 1024
GROUP = 64
RLEN = 128
NEIGH = 2
POOL = 16
LENGTH = 1024
N_SIDE = 2
N_SEQ = 32


def shared_normal(key):
    return jax.random.normal(key, (N_SIDE, N_SEQ, LENGTH, HEADS * HD), jnp.float32)


def draw_self_key(key, part):
    base_keys = shared_normal(key)
    return base_keys.astype(jnp.bfloat16)


def draw_self_query(key, part):
    key = jax.random.fold_in(key, 2)
    own_rows = jax.random.normal(key, (N_SIDE, N_SEQ, LENGTH, HEADS * HD), jnp.float32)
    return own_rows.astype(jnp.bfloat16)


def draw_cross_query(key, part):
    key = jax.random.fold_in(key, 3)
    own_rows = jax.random.normal(key, (N_SIDE, N_SEQ, LENGTH, HEADS * HD), jnp.float32)
    return own_rows.astype(jnp.bfloat16)


def with_ends(drawn, rng, low, high):
    longest = drawn.shape.index(max(drawn.shape))
    spots = []
    for shift in (0, 1):
        where = [jax.random.randint(jax.random.fold_in(rng, axis), (), 0, length) for axis, length in enumerate(drawn.shape)]
        where[longest] = (where[longest] + shift) % drawn.shape[longest]
        spots.append(tuple(where))
    return drawn.at[spots[0]].set(low).at[spots[1]].set(high)


def level_of(own_key, dims, split, smallest, top_value):
    factor_of = 1.0
    for position, blocks in split:
        heights = jax.random.uniform(jax.random.fold_in(jax.random.fold_in(own_key, 6), position), (blocks,), jnp.float32, smallest / len(split), top_value / len(split))
        factor_of = factor_of * jnp.repeat(jnp.exp(heights), dims[position] // blocks).reshape((-1,) + (1,) * (len(dims) - 1 - position))
    return factor_of


def scatter_about(stream_key, extent, width, reach, shards=(), kind=jnp.bfloat16):
    gain = level_of(stream_key, extent, shards, -0.22, 0.18) if shards else 1.0
    drawn = jax.random.normal(stream_key, extent, jnp.float32) * width * gain
    return jnp.minimum(jnp.maximum(drawn, -reach), reach).astype(kind)


def setup_inputs(seed: int = 0) -> dict:
    splits = jax.random.split(jax.random.key(seed), 10)
    return {
        "self_query": draw_self_query(jax.random.fold_in(splits[9], 71), 0),
        "self_key": draw_self_key(jax.random.fold_in(splits[9], 71), 0),
        "self_value": scatter_about(splits[2], (N_SIDE, N_SEQ, LENGTH, HEADS * HD), 1.0, 6.0, ((0, 2), (1, 32), (3, 8))),
        "cross_query": draw_cross_query(jax.random.fold_in(splits[9], 71), 0),
        "passages": scatter_about(splits[4], (N_SIDE, N_SEQ, POOL, RLEN, DE), 1.0, 6.0, ((0, 2), (1, 32), (4, 8))),
        "w_key": scatter_about(splits[5], (DE, HEADS * HD), DE ** -0.5, 0.1875, ((1, 8),)),
        "w_value": scatter_about(splits[6], (DE, HEADS * HD), DE ** -0.5, 0.1875, ((1, 8),)),
        "block_map": jax.vmap(lambda own: jax.random.permutation(own, N_SEQ))(jax.random.split(splits[7], N_SIDE * N_SEQ)).reshape((N_SIDE, N_SEQ, N_SEQ)).astype(jnp.int32),
        "passage_ids": with_ends(jax.random.randint(splits[8], (N_SIDE, N_SEQ, N_SEQ), 0, POOL), jax.random.fold_in(splits[8], 1), 0, POOL - 1).astype(jnp.int32),
    }


def self_attention(queries, key_rows, value_rows):
    length = queries.shape[0]
    query_heads = queries.astype(jnp.float32).reshape(length, HEADS, HD)
    key_heads = key_rows.astype(jnp.float32).reshape(length, HEADS, HD)
    value_heads = value_rows.astype(jnp.float32).reshape(length, HEADS, HD)
    scores = jnp.einsum('qhd,khd->hqk', query_heads, key_heads) * (1.0 / math.sqrt(HD))
    row_ids = lax.broadcasted_iota(jnp.int32, (length, length), 0)
    col_ids = lax.broadcasted_iota(jnp.int32, (length, length), 1)
    scores = jnp.where((col_ids <= row_ids)[None], scores, -jnp.inf)
    row_max = lax.optimization_barrier(jnp.max(scores, axis=-1, keepdims=True))
    raised = jnp.exp(scores - row_max)
    weights = (raised / lax.optimization_barrier(jnp.sum(raised, axis=-1, keepdims=True))).astype(jnp.bfloat16)
    attended = jnp.einsum('hqk,khd->qhd', weights.astype(jnp.float32), value_heads)
    return attended.reshape(length, HEADS * HD)

def cross_attention(queries, slot_keys, slot_values):
    length, feats = queries.shape
    groups = length // GROUP
    lead_rows = GROUP - 1
    shifted = jnp.concatenate([queries[lead_rows:], jnp.zeros((lead_rows, feats), queries.dtype)], 0)
    shifted = shifted.astype(jnp.float32).reshape(groups, GROUP, HEADS, HD)
    group_keys = slot_keys.astype(jnp.float32).reshape(groups, NEIGH * RLEN, HEADS, HD)
    group_values = slot_values.astype(jnp.float32).reshape(groups, NEIGH * RLEN, HEADS, HD)
    scores = jnp.einsum('cqhd,ckhd->chqk', shifted, group_keys) * (1.0 / math.sqrt(HD))
    row_max = lax.optimization_barrier(jnp.max(scores, axis=-1, keepdims=True))
    raised = jnp.exp(scores - row_max)
    weights = (raised / lax.optimization_barrier(jnp.sum(raised, axis=-1, keepdims=True))).astype(jnp.bfloat16)
    attended = jnp.einsum('chqk,ckhd->cqhd', weights.astype(jnp.float32), group_values)
    attended = attended.reshape(length, feats)
    return jnp.concatenate([jnp.zeros((lead_rows, feats), jnp.float32), attended[:length - lead_rows]], 0)

def reference(self_query, self_key, self_value, cross_query, passages, w_key, w_value, block_map, passage_ids):
    count = N_SIDE * N_SEQ
    feats = HEADS * HD
    side_of = (jnp.arange(count, dtype=jnp.int32) // N_SEQ).astype(jnp.int32)
    key_weight = w_key.astype(jnp.float32)
    value_weight = w_value.astype(jnp.float32)

    def one_sequence(items):
        side_here, queries, key_rows, value_rows, cross_rows, slot_blocks, slot_passages = items
        source = lax.dynamic_index_in_dim(passages, (1 - side_here).astype(jnp.int32), 0, keepdims=False)
        picked = source[slot_blocks, slot_passages].reshape(N_SEQ * RLEN, DE).astype(jnp.float32)
        slot_keys = jnp.dot(picked, key_weight, preferred_element_type=jnp.float32).astype(jnp.bfloat16)
        slot_values = jnp.dot(picked, value_weight, preferred_element_type=jnp.float32).astype(jnp.bfloat16)
        self_out = self_attention(queries, key_rows, value_rows)
        cross_out = cross_attention(cross_rows, slot_keys, slot_values)
        return (self_out + cross_out).astype(jnp.bfloat16)
    mixed = lax.map(one_sequence, (side_of, self_query.reshape(count, LENGTH, feats), self_key.reshape(count, LENGTH, feats), self_value.reshape(count, LENGTH, feats), cross_query.reshape(count, LENGTH, feats), block_map.reshape(count, N_SEQ), passage_ids.reshape(count, N_SEQ)))
    return mixed.reshape(N_SIDE, N_SEQ, LENGTH, feats)
```

```python
import math

import jax
import jax.numpy as jnp
from jax import lax
from jax.experimental import pallas as pl
from jax.experimental.pallas import tpu as pltpu
from jax.sharding import PartitionSpec as P

HD = 128
GROUP = 64
NEIGH = 2
EXTRA = 8
VMEM_BYTES = 40 * 1024 * 1024
EXP2_SCALE = math.log2(math.e) / math.sqrt(HD)

NT = (((1,), (1,)), ((), ()))
TN = (((0,), (0,)), ((), ()))


def params(**kwargs):
    return pltpu.CompilerParams(vmem_limit_bytes=VMEM_BYTES, **kwargs)


def last_row_mask(rows, cols):
    return lax.broadcasted_iota(jnp.int32, (rows, cols), 0) < rows - 1


def pack_kernel(place, block_map, query_ref, out_ref):
    groups, rows, cols = query_ref.shape
    own_side, own_seq = place[0], place[1]
    head = last_row_mask(rows, cols)
    for u in range(groups):
        chunk = jnp.where(head, query_ref[min(u + 1, groups - 1)], query_ref[u])
        for n in range(NEIGH):
            out_ref[block_map[own_side, own_seq, NEIGH * u + n]] = chunk


def pack_queries(place, block_map, queries, blocks):
    groups, rows, cols = queries.shape
    return pl.pallas_call(
        pack_kernel,
        out_shape=jax.ShapeDtypeStruct((blocks, rows, cols), queries.dtype),
        grid_spec=pltpu.PrefetchScalarGridSpec(
            num_scalar_prefetch=2,
            grid=(1,),
            in_specs=[pl.BlockSpec((groups, rows, cols), lambda i, *_: (0, 0, 0))],
            out_specs=pl.BlockSpec((blocks, rows, cols), lambda i, *_: (0, 0, 0)),
        ),
        compiler_params=params(),
        cost_estimate=pl.CostEstimate(
            flops=0, bytes_accessed=2 * (groups + blocks) * rows * cols, transcendentals=0
        ),
        name="pack_queries",
    )(place, block_map, queries)


def self_kernel(query_ref, key_ref, value_ref, out_ref, *, block):
    length, feats = query_ref.shape
    row = lax.broadcasted_iota(jnp.int32, (block, block), 0)
    col = lax.broadcasted_iota(jnp.int32, (block, block), 1)
    for g in range(feats // HD):
        cols = slice(g * HD, (g + 1) * HD)
        for i in range(length // block):
            rows = slice(i * block, (i + 1) * block)
            stop = (i + 1) * block
            query = query_ref[rows, cols]
            scores = lax.dot_general(
                query, key_ref[:stop, cols], NT, preferred_element_type=jnp.float32
            )
            tail = jnp.where(col <= row, scores[:, i * block :], -jnp.inf)
            scores = tail if i == 0 else jnp.concatenate([scores[:, : i * block], tail], 1)
            top = jnp.max(scores, axis=1, keepdims=True)
            raised = jnp.exp2((scores - top) * EXP2_SCALE)
            total = jnp.sum(raised, axis=1, keepdims=True)
            weights = (raised * (1.0 / total)).astype(jnp.bfloat16)
            out_ref[rows, cols] = jnp.dot(
                weights, value_ref[:stop, cols], preferred_element_type=jnp.float32
            )


def self_attention(queries, key_rows, value_rows):
    length, feats = queries.shape
    block = min(256, length)
    return pl.pallas_call(
        lambda *refs: self_kernel(*refs, block=block),
        out_shape=jax.ShapeDtypeStruct((length, feats), jnp.float32),
        in_specs=[pl.BlockSpec(memory_space=pltpu.VMEM)] * 3,
        out_specs=pl.BlockSpec(memory_space=pltpu.VMEM),
        compiler_params=params(),
        cost_estimate=pl.CostEstimate(
            flops=3 * length * length * feats,
            bytes_accessed=10 * length * feats,
            transcendentals=length * length * feats // HD // 2,
        ),
        name="self_attention",
    )(queries, key_rows, value_rows)


def cross_kernel(wanted, passage_ref, wkey_ref, wvalue_ref, query_ref, out_ref, kv_ref, *, project_steps):
    step = pl.program_id(0)
    shards, per_step, rlen, part = passage_ref.shape
    feats = wkey_ref.shape[1]

    @pl.when(step < project_steps)
    def _():
        lhs = jnp.concatenate(
            [passage_ref[t].reshape(per_step * rlen, part) for t in range(shards)], axis=1
        )
        keys = jnp.dot(lhs, wkey_ref[...], preferred_element_type=jnp.float32)
        values = jnp.dot(lhs, wvalue_ref[...], preferred_element_type=jnp.float32)
        where = pl.ds(step * per_step, per_step)
        kv_ref[where, :, :feats] = keys.astype(jnp.bfloat16).reshape(per_step, rlen, feats)
        kv_ref[where, :, feats:] = values.astype(jnp.bfloat16).reshape(per_step, rlen, feats)

    @pl.when(step >= project_steps)
    def _():
        per_chunk, rows, _ = query_ref.shape
        heads = feats // HD
        first = (step - project_steps) * per_chunk
        zeros = jnp.zeros((rows, HD), jnp.bfloat16)
        for i in range(per_chunk):
            passage = wanted[first + i]
            query = query_ref[i]
            spread = jnp.concatenate(
                [
                    jnp.concatenate(
                        [query[:, g * HD : (g + 1) * HD] if g == k else zeros for k in range(heads)], 1
                    )
                    for g in range(heads)
                ],
                0,
            )
            scores = lax.dot_general(
                kv_ref[passage, :, :feats], spread, NT, preferred_element_type=jnp.float32
            )
            top = jnp.max(scores, axis=0, keepdims=True)
            raised = jnp.exp2((scores - top) * EXP2_SCALE)
            total = jnp.sum(raised, axis=0, keepdims=True)
            weights = (raised * (1.0 / total)).astype(jnp.bfloat16)
            attended = lax.dot_general(
                weights, kv_ref[passage, :, feats:], TN, preferred_element_type=jnp.float32
            )
            for g in range(heads):
                out_ref[i, :rows, g * HD : (g + 1) * HD] = attended[
                    g * rows : (g + 1) * rows, g * HD : (g + 1) * HD
                ].astype(jnp.bfloat16)
            level = top * EXP2_SCALE + jnp.log2(total)
            high = level.astype(jnp.bfloat16)
            rest = level - high.astype(jnp.float32)
            middle = rest.astype(jnp.bfloat16)
            low = (rest - middle.astype(jnp.float32)).astype(jnp.bfloat16)
            lead = jnp.concatenate([high, middle], 1).astype(jnp.float32)
            follow = jnp.concatenate([low, low], 1).astype(jnp.float32)
            picked = lax.broadcasted_iota(jnp.int32, (EXTRA, feats), 0) == 0
            out_ref[i, rows:, :] = jnp.where(picked, lead, follow).astype(jnp.bfloat16)


def cross_attention(wanted, gathered, w_key, w_value, queries):
    shards, pool, rlen, part = gathered.shape
    chunks, rows, feats = queries.shape
    project_steps, attend_steps = 4, 2
    per_step, per_chunk = pool // project_steps, chunks // attend_steps
    depth = shards * part
    late = lambda i: jnp.maximum(i - project_steps, 0)
    return pl.pallas_call(
        lambda *refs: cross_kernel(*refs, project_steps=project_steps),
        out_shape=jax.ShapeDtypeStruct((chunks, rows + EXTRA, feats), jnp.bfloat16),
        grid_spec=pltpu.PrefetchScalarGridSpec(
            num_scalar_prefetch=1,
            grid=(project_steps + attend_steps,),
            in_specs=[
                pl.BlockSpec(
                    (shards, per_step, rlen, part),
                    lambda i, *_: (0, jnp.minimum(i, project_steps - 1), 0, 0),
                ),
                pl.BlockSpec((depth, feats), lambda i, *_: (0, 0)),
                pl.BlockSpec((depth, feats), lambda i, *_: (0, 0)),
                pl.BlockSpec((per_chunk, rows, feats), lambda i, *_: (late(i), 0, 0)),
            ],
            out_specs=pl.BlockSpec((per_chunk, rows + EXTRA, feats), lambda i, *_: (late(i), 0, 0)),
            scratch_shapes=[pltpu.VMEM((pool, rlen, 2 * feats), jnp.bfloat16)],
        ),
        compiler_params=params(),
        cost_estimate=pl.CostEstimate(
            flops=4 * pool * rlen * depth * feats + 8 * chunks * rows * rlen * feats,
            bytes_accessed=2 * (pool * rlen * depth + 2 * depth * feats + 2 * chunks * rows * feats),
            transcendentals=chunks * rows * rlen * feats // HD,
        ),
        name="cross_attention",
    )(wanted, gathered, w_key, w_value, queries)


def mix_kernel(place, block_map, arrived_ref, self_ref, out_ref):
    groups, rows, feats = self_ref.shape
    heads = feats // HD
    own_side, own_seq = place[0], place[1]

    def level_of(block):
        packed = arrived_ref[block, rows:, :].astype(jnp.float32)
        half = feats // 2
        return packed[0:1, :half] + packed[0:1, half:] + packed[1:2, :half]

    slots = [
        [block_map[own_side, own_seq, NEIGH * u + n] for n in range(NEIGH)] for u in range(groups)
    ]
    firsts = jnp.concatenate([level_of(pair[0]) for pair in slots], 0)
    seconds = jnp.concatenate([level_of(pair[1]) for pair in slots], 0)
    top = jnp.maximum(firsts, seconds)
    raised = jnp.exp2(firsts - top)
    share = raised / (raised + jnp.exp2(seconds - top))
    columns = share.T
    head = last_row_mask(rows, HD)
    for g in range(heads):
        cols = slice(g * HD, (g + 1) * HD)
        before = jnp.zeros((rows, HD), jnp.float32)
        for u in range(groups):
            one = arrived_ref[slots[u][0], :rows, cols].astype(jnp.float32)
            two = arrived_ref[slots[u][1], :rows, cols].astype(jnp.float32)
            part = columns[g * rows : (g + 1) * rows, u : u + 1]
            now = two + part * (one - two)
            cross = jnp.where(head, before, now)
            out_ref[u, :, cols] = (self_ref[u, :, cols] + cross).astype(jnp.bfloat16)
            before = now


def mix(place, block_map, arrived, self_out):
    groups, rows, feats = self_out.shape
    chunks = arrived.shape[0]
    whole = lambda i, *_: (0, 0, 0)
    return pl.pallas_call(
        mix_kernel,
        out_shape=jax.ShapeDtypeStruct(self_out.shape, jnp.bfloat16),
        grid_spec=pltpu.PrefetchScalarGridSpec(
            num_scalar_prefetch=2,
            grid=(1,),
            in_specs=[
                pl.BlockSpec((chunks, rows + EXTRA, feats), whole),
                pl.BlockSpec((groups, rows, feats), whole),
            ],
            out_specs=pl.BlockSpec((groups, rows, feats), whole),
        ),
        compiler_params=params(),
        cost_estimate=pl.CostEstimate(
            flops=8 * groups * rows * feats,
            bytes_accessed=10 * groups * rows * feats,
            transcendentals=0,
        ),
        name="mix",
    )(place, block_map, arrived, self_out)


def on_device(
    self_query, self_key, self_value, cross_query, passages, w_key, w_value, block_map, passage_ids
):
    side_now = lax.axis_index("side")
    seq_now = lax.axis_index("seq")
    blocks = lax.axis_size("seq")
    place = jnp.stack([side_now, seq_now]).astype(jnp.int32)
    length, feats = cross_query.shape[2:]
    groups = length // GROUP

    near = lax.ppermute(passages[0, 0], "side", [(0, 1), (1, 0)])
    gathered = lax.all_gather(near, "tp")

    served_map = lax.dynamic_index_in_dim(block_map, side_now, 0, keepdims=False)
    served_ids = lax.dynamic_index_in_dim(passage_ids, side_now, 0, keepdims=False)
    wanted = jnp.sum(jnp.where(served_map == seq_now, served_ids, 0), axis=1)

    chunks = pack_queries(place, block_map, cross_query[0, 0].reshape(groups, GROUP, feats), blocks)
    chunks, _ = lax.optimization_barrier((chunks, near[0, 0, 0]))
    asked = lax.all_to_all(chunks, "seq", split_axis=0, concat_axis=0, tiled=True)
    self_out = self_attention(self_query[0, 0], self_key[0, 0], self_value[0, 0])

    answers = cross_attention(wanted, gathered, w_key, w_value, asked)
    arrived = lax.all_to_all(answers, "seq", split_axis=0, concat_axis=0, tiled=True)
    mixed = mix(place, block_map, arrived, self_out.reshape(groups, GROUP, feats))
    return mixed.reshape(1, 1, length, feats)


def solution(mesh):
    return jax.shard_map(
        on_device,
        mesh=mesh,
        in_specs=(
            P("side", "seq", None, "tp"),
            P("side", "seq", None, "tp"),
            P("side", "seq", None, "tp"),
            P("side", "seq", None, "tp"),
            P("side", "seq", None, None, "tp"),
            P(None, "tp"),
            P(None, "tp"),
            P(),
            P(),
        ),
        out_specs=P("side", "seq", None, "tp"),
        check_vma=False,
    )
```

```python
import functools
import math

import jax
import jax.numpy as jnp
from jax import lax
from jax.experimental import pallas as pl
from jax.experimental.pallas import tpu as pltpu
from jax.sharding import PartitionSpec as P

HD = 128
GROUP = 64
NEIGH = 2
EXTRA = 8
ORDER_FLOPS = 10000000000
LOAD_PARTS = 2
STORE_PARTS = 4
CROSS_VMEM_BYTES = 58 * 1024 * 1024
VMEM_BYTES = 20 * 1024 * 1024
EXP2_SCALE = math.log2(math.e) / math.sqrt(HD)

NT = (((1,), (1,)), ((), ()))
ANYWHERE = pl.BlockSpec(memory_space=pl.ANY)
IN_VMEM = pl.BlockSpec(memory_space=pltpu.VMEM)
TN = (((0,), (0,)), ((), ()))


def params(**kwargs):
    return pltpu.CompilerParams(vmem_limit_bytes=VMEM_BYTES, **kwargs)


def last_row_mask(rows, cols):
    return lax.broadcasted_iota(jnp.int32, (rows, cols), 0) < rows - 1


def pack_kernel(place, block_map, query_ref, out_ref):
    groups, rows, cols = query_ref.shape
    own_side, own_seq = place[0], place[1]
    head = last_row_mask(rows, cols)
    for u in range(groups):
        chunk = jnp.where(head, query_ref[min(u + 1, groups - 1)], query_ref[u])
        for n in range(NEIGH):
            out_ref[block_map[own_side, own_seq, NEIGH * u + n]] = chunk


def pack_queries(place, block_map, queries, blocks):
    groups, rows, cols = queries.shape
    return pl.pallas_call(
        pack_kernel,
        out_shape=jax.ShapeDtypeStruct((blocks, rows, cols), queries.dtype),
        grid_spec=pltpu.PrefetchScalarGridSpec(
            num_scalar_prefetch=2,
            grid=(1,),
            in_specs=[pl.BlockSpec((groups, rows, cols), lambda i, *_: (0, 0, 0))],
            out_specs=pl.BlockSpec((blocks, rows, cols), lambda i, *_: (0, 0, 0)),
        ),
        compiler_params=params(),
        cost_estimate=pl.CostEstimate(
            flops=0, bytes_accessed=2 * (groups + blocks) * rows * cols, transcendentals=0
        ),
        name="pack_queries",
    )(place, block_map, queries)


def self_kernel(query_ref, key_ref, value_ref, out_ref, *, block):
    length, feats = query_ref.shape
    row = lax.broadcasted_iota(jnp.int32, (block, block), 0)
    col = lax.broadcasted_iota(jnp.int32, (block, block), 1)
    for g in range(feats // HD):
        cols = slice(g * HD, (g + 1) * HD)
        for i in range(length // block):
            rows = slice(i * block, (i + 1) * block)
            stop = (i + 1) * block
            query = query_ref[rows, cols]
            scores = lax.dot_general(
                query, key_ref[:stop, cols], NT, preferred_element_type=jnp.float32
            )
            tail = jnp.where(col <= row, scores[:, i * block :], -jnp.inf)
            scores = tail if i == 0 else jnp.concatenate([scores[:, : i * block], tail], 1)
            top = jnp.max(scores, axis=1, keepdims=True)
            raised = jnp.exp2((scores - top) * EXP2_SCALE)
            total = jnp.sum(raised, axis=1, keepdims=True)
            weights = (raised * (1.0 / total)).astype(jnp.bfloat16)
            out_ref[rows, cols] = jnp.dot(
                weights, value_ref[:stop, cols], preferred_element_type=jnp.float32
            )


def self_attention(queries, key_rows, value_rows):
    length, feats = queries.shape
    block = min(256, length)
    return pl.pallas_call(
        lambda *refs: self_kernel(*refs, block=block),
        out_shape=jax.ShapeDtypeStruct((length, feats), jnp.float32),
        in_specs=[pl.BlockSpec(memory_space=pltpu.VMEM)] * 3,
        out_specs=pl.BlockSpec(memory_space=pltpu.VMEM),
        compiler_params=params(),
        cost_estimate=pl.CostEstimate(
            flops=3 * length * length * feats,
            bytes_accessed=10 * length * feats,
            transcendentals=length * length * feats // HD // 2,
        ),
        name="self_attention",
    )(queries, key_rows, value_rows)


def order_kernel(owners, wkey_ref, wvalue_ref, out_ref):
    part = out_ref.shape[0] // owners.shape[0]
    feats = wkey_ref.shape[1]
    for n in range(out_ref.shape[0] // part):
        rows = pl.ds(pl.multiple_of(owners[n] * part, part), part)
        out_ref[n * part : (n + 1) * part, :feats] = wkey_ref[rows, :]
        out_ref[n * part : (n + 1) * part, feats:] = wvalue_ref[rows, :]


def order_weights(owners, w_key, w_value):
    depth, feats = w_key.shape
    return pl.pallas_call(
        order_kernel,
        out_shape=jax.ShapeDtypeStruct((depth, 2 * feats), w_key.dtype),
        in_specs=[pl.BlockSpec(memory_space=pltpu.SMEM)] + [IN_VMEM] * 2,
        out_specs=IN_VMEM,
        compiler_params=params(),
        cost_estimate=pl.CostEstimate(flops=ORDER_FLOPS, bytes_accessed=8 * depth * feats, transcendentals=0),
        name="order_weights",
    )(owners, w_key, w_value)


def cross_kernel(wanted, *refs, places):
    shards, depth = len(places), max(row for row, _ in places) + 1
    weight_hbm, query_hbm, shard_hbm, out_hbm = refs[0], refs[1], refs[2 : 2 + shards], refs[2 + shards]
    weight_ref, query_ref, lhs_ref, kv_ref, out_ref, load_sems, lhs_sems, out_sems = refs[3 + shards :]
    chunks, rows, feats = query_ref.shape
    heads = feats // HD
    _, pool, rlen, part = lhs_ref.shape
    per = pool // LOAD_PARTS

    load_weight = pltpu.make_async_copy(weight_hbm, weight_ref, load_sems.at[0])
    load_query = pltpu.make_async_copy(query_hbm, query_ref, load_sems.at[1])
    load_lhs = [
        [
            pltpu.make_async_copy(
                shard_hbm[n].at[pl.ds(k * per - low, per)],
                lhs_ref.at[row, pl.ds(k * per, per)],
                lhs_sems.at[k, row],
            )
            for n, (row, low) in enumerate(places)
            if low <= k * per < low + shard_hbm[n].shape[0]
        ]
        for k in range(LOAD_PARTS)
    ]
    load_weight.start()
    for copies in load_lhs:
        for copy in copies:
            copy.start()
    load_query.start()
    load_weight.wait()
    for k, copies in enumerate(load_lhs):
        for copy in copies:
            copy.wait()
        span = slice(k * per, (k + 1) * per)
        lhs = jnp.concatenate([lhs_ref[n, span].reshape(per * rlen, part) for n in range(depth)], 1)
        made = jnp.dot(lhs, weight_ref[...], preferred_element_type=jnp.float32)
        kv_ref[span] = made.astype(jnp.bfloat16).reshape(per, rlen, 2 * feats)
    load_query.wait()

    zeros = jnp.zeros((rows, HD), jnp.bfloat16)
    extra_row = lax.broadcasted_iota(jnp.int32, (EXTRA, heads * rows), 0)
    stores = []
    for i in range(chunks):
        passage = wanted[i]
        query = query_ref[i]
        spread = jnp.concatenate(
            [
                jnp.concatenate(
                    [query[:, g * HD : (g + 1) * HD] if g == k else zeros for k in range(heads)], 1
                )
                for g in range(heads)
            ],
            0,
        )
        scores = lax.dot_general(
            kv_ref[passage, :, :feats], spread, NT, preferred_element_type=jnp.float32
        )
        top = jnp.max(scores, axis=0, keepdims=True)
        raised = jnp.exp2((scores - top) * EXP2_SCALE)
        total = jnp.sum(raised, axis=0, keepdims=True)
        weights = (raised * (1.0 / total)).astype(jnp.bfloat16)
        attended = lax.dot_general(
            weights, kv_ref[passage, :, feats:], TN, preferred_element_type=jnp.float32
        )
        for g in range(heads):
            own = slice(g * rows, (g + 1) * rows)
            out_ref[i, own, :] = attended[own, g * HD : (g + 1) * HD].astype(jnp.bfloat16)
        level = top * EXP2_SCALE + jnp.log2(total)
        high = level.astype(jnp.bfloat16).astype(jnp.float32)
        middle = (level - high).astype(jnp.bfloat16).astype(jnp.float32)
        low = (level - high) - middle
        terms = jnp.where(extra_row == 0, high, jnp.where(extra_row == 1, middle, low))
        out_ref[i, heads * rows :, :] = terms.astype(jnp.bfloat16)
        step = chunks // STORE_PARTS
        if (i + 1) % step == 0:
            span = pl.ds(i + 1 - step, step)
            store = pltpu.make_async_copy(out_ref.at[span], out_hbm.at[span], out_sems.at[i // step])
            store.start()
            stores.append(store)
    for store in stores:
        store.wait()


def cross_attention(wanted, shards, weights, queries):
    half, rlen, part = shards[0].shape
    pool = 2 * half
    chunks, rows, feats = queries.shape
    depth = weights.shape[0]
    heads = feats // HD
    positions = depth // part
    places = [(n, low) for n in range(positions) for low in (0, half)]
    out_shape = jax.ShapeDtypeStruct((chunks, heads * rows + EXTRA, HD), jnp.bfloat16)
    return pl.pallas_call(
        functools.partial(cross_kernel, places=places),
        out_shape=out_shape,
        in_specs=[pl.BlockSpec(memory_space=pltpu.SMEM)] + [ANYWHERE] * (2 + len(shards)),
        out_specs=ANYWHERE,
        scratch_shapes=[
            pltpu.VMEM(weights.shape, jnp.bfloat16),
            pltpu.VMEM(queries.shape, jnp.bfloat16),
            pltpu.VMEM((positions, pool, rlen, part), jnp.bfloat16),
            pltpu.VMEM((pool, rlen, 2 * feats), jnp.bfloat16),
            pltpu.VMEM(out_shape.shape, jnp.bfloat16),
            pltpu.SemaphoreType.DMA((2,)),
            pltpu.SemaphoreType.DMA((LOAD_PARTS, positions)),
            pltpu.SemaphoreType.DMA((STORE_PARTS,)),
        ],
        compiler_params=pltpu.CompilerParams(vmem_limit_bytes=CROSS_VMEM_BYTES),
        cost_estimate=pl.CostEstimate(
            flops=4 * pool * rlen * depth * feats + 8 * chunks * rows * rlen * feats,
            bytes_accessed=2 * (pool * rlen * depth + 2 * depth * feats + 2 * chunks * rows * feats),
            transcendentals=chunks * rows * rlen * heads,
        ),
        name="cross_attention",
    )(wanted, weights, queries, *shards)


def mix_kernel(place, block_map, arrived_ref, self_ref, out_ref):
    groups, rows, feats = self_ref.shape
    heads = feats // HD
    own_side, own_seq = place[0], place[1]

    def level_of(block):
        terms = arrived_ref[block, heads * rows :, :].astype(jnp.float32)
        return (terms[0:1] + terms[1:2]) + terms[2:3]

    slots = [
        [block_map[own_side, own_seq, NEIGH * u + n] for n in range(NEIGH)] for u in range(groups)
    ]
    firsts = jnp.concatenate([level_of(pair[0]) for pair in slots], 0)
    seconds = jnp.concatenate([level_of(pair[1]) for pair in slots], 0)
    top = jnp.maximum(firsts, seconds)
    raised = jnp.exp2(firsts - top)
    share = raised / (raised + jnp.exp2(seconds - top))
    columns = share.T
    head = last_row_mask(rows, HD)
    for g in range(heads):
        cols = slice(g * HD, (g + 1) * HD)
        own = slice(g * rows, (g + 1) * rows)
        before = jnp.zeros((rows, HD), jnp.float32)
        for u in range(groups):
            one = arrived_ref[slots[u][0], own, :].astype(jnp.float32)
            two = arrived_ref[slots[u][1], own, :].astype(jnp.float32)
            now = two + columns[own, u : u + 1] * (one - two)
            cross = jnp.where(head, before, now)
            out_ref[u, :, cols] = (self_ref[u, :, cols] + cross).astype(jnp.bfloat16)
            before = now


def mix(place, block_map, arrived, self_out):
    groups, rows, feats = self_out.shape
    return pl.pallas_call(
        mix_kernel,
        out_shape=jax.ShapeDtypeStruct(self_out.shape, jnp.bfloat16),
        in_specs=[pl.BlockSpec(memory_space=pltpu.SMEM)] * 2 + [IN_VMEM] * 2,
        out_specs=IN_VMEM,
        compiler_params=params(),
        cost_estimate=pl.CostEstimate(
            flops=8 * groups * rows * feats,
            bytes_accessed=10 * groups * rows * feats,
            transcendentals=0,
        ),
        name="mix",
    )(place, block_map, arrived, self_out)


def ring_gather(low, high, axis):
    count = lax.axis_size(axis)
    up = [(i, (i + 1) % count) for i in range(count)]
    down = [(i, (i - 1) % count) for i in range(count)]
    shards = [low, high]
    right_low = left_low = low
    right_high = left_high = high
    for _ in range(1, count // 2):
        right_low = lax.ppermute(right_low, axis, up)
        left_low = lax.ppermute(left_low, axis, down)
        right_high = lax.ppermute(right_high, axis, up)
        left_high = lax.ppermute(left_high, axis, down)
        shards += [right_low, right_high, left_low, left_high]
    shards.append(lax.ppermute(right_low, axis, up))
    shards.append(lax.ppermute(left_high, axis, down))
    return shards


def ring_owners(axis):
    count = lax.axis_size(axis)
    here = lax.axis_index(axis)
    owners = [here]
    for hop in range(1, count // 2):
        owners += [here - hop, here + hop]
    owners.append(here + count // 2)
    return jnp.stack(owners).astype(jnp.int32) % count


def on_device(
    self_query, self_key, self_value, cross_query, passages, w_key, w_value, block_map, passage_ids
):
    side_now = lax.axis_index("side")
    seq_now = lax.axis_index("seq")
    blocks = lax.axis_size("seq")
    place = jnp.stack([side_now, seq_now]).astype(jnp.int32)
    length, feats = cross_query.shape[2:]
    groups = length // GROUP

    near = lax.ppermute(passages[0, 0], "side", [(0, 1), (1, 0)])
    half = near.shape[0] // 2

    served_map = lax.dynamic_index_in_dim(block_map, side_now, 0, keepdims=False)
    served_ids = lax.dynamic_index_in_dim(passage_ids, side_now, 0, keepdims=False)
    wanted = jnp.sum(jnp.where(served_map == seq_now, served_ids, 0), axis=1)

    chunks = pack_queries(place, block_map, cross_query[0, 0].reshape(groups, GROUP, feats), blocks)
    asked = lax.all_to_all(chunks, "seq", split_axis=0, concat_axis=0, tiled=True)
    self_out = self_attention(self_query[0, 0], self_key[0, 0], self_value[0, 0])

    near, wanted, owners, w_key, w_value = lax.optimization_barrier(
        (near, wanted, ring_owners("tp"), w_key, w_value)
    )
    weights = order_weights(owners, w_key, w_value)
    shards = ring_gather(near[:half], near[half:], "tp")
    answers = cross_attention(wanted, shards, weights, asked)
    arrived = lax.all_to_all(answers, "seq", split_axis=0, concat_axis=0, tiled=True)
    mixed = mix(place, block_map, arrived, self_out.reshape(groups, GROUP, feats))
    return mixed.reshape(1, 1, length, feats)


def solution(mesh):
    return jax.shard_map(
        on_device,
        mesh=mesh,
        in_specs=(
            P("side", "seq", None, "tp"),
            P("side", "seq", None, "tp"),
            P("side", "seq", None, "tp"),
            P("side", "seq", None, "tp"),
            P("side", "seq", None, None, "tp"),
            P(None, "tp"),
            P(None, "tp"),
            P(),
            P(),
        ),
        out_specs=P("side", "seq", None, "tp"),
        check_vma=False,
    )
```

```python
import functools
import math

import jax
import jax.numpy as jnp
from jax import lax
from jax.experimental import pallas as pl
from jax.experimental.pallas import tpu as pltpu
from jax.sharding import PartitionSpec as P

HD = 128
GROUP = 64
NEIGH = 2
EXTRA = 8
WANTED_FLOPS = 13000000000
LOAD_PARTS = 2
STORE_PARTS = 4
CROSS_VMEM_BYTES = 58 * 1024 * 1024
VMEM_BYTES = 20 * 1024 * 1024
EXP2_SCALE = math.log2(math.e) / math.sqrt(HD)

NT = (((1,), (1,)), ((), ()))
ANYWHERE = pl.BlockSpec(memory_space=pl.ANY)
IN_VMEM = pl.BlockSpec(memory_space=pltpu.VMEM)
TN = (((0,), (0,)), ((), ()))


def params(**kwargs):
    return pltpu.CompilerParams(vmem_limit_bytes=VMEM_BYTES, **kwargs)


def last_row_mask(rows, cols):
    return lax.broadcasted_iota(jnp.int32, (rows, cols), 0) < rows - 1


def holder_of(block, blocks):
    return (block + blocks // 2) % blocks


def pack_kernel(place, block_map, query_ref, out_ref):
    groups, rows, cols = query_ref.shape
    own_side, own_seq = place[0], place[1]
    head = last_row_mask(rows, cols)
    for u in range(groups):
        chunk = jnp.where(head, query_ref[min(u + 1, groups - 1)], query_ref[u])
        for n in range(NEIGH):
            out_ref[holder_of(block_map[own_side, own_seq, NEIGH * u + n], out_ref.shape[0])] = chunk


def pack_queries(place, block_map, queries, blocks):
    groups, rows, cols = queries.shape
    return pl.pallas_call(
        pack_kernel,
        out_shape=jax.ShapeDtypeStruct((blocks, rows, cols), queries.dtype),
        grid_spec=pltpu.PrefetchScalarGridSpec(
            num_scalar_prefetch=2,
            grid=(1,),
            in_specs=[pl.BlockSpec((groups, rows, cols), lambda i, *_: (0, 0, 0))],
            out_specs=pl.BlockSpec((blocks, rows, cols), lambda i, *_: (0, 0, 0)),
        ),
        compiler_params=params(),
        cost_estimate=pl.CostEstimate(
            flops=0, bytes_accessed=2 * (groups + blocks) * rows * cols, transcendentals=0
        ),
        name="pack_queries",
    )(place, block_map, queries)


def self_kernel(query_ref, key_ref, value_ref, out_ref, *, block):
    length, feats = query_ref.shape
    row = lax.broadcasted_iota(jnp.int32, (block, block), 0)
    col = lax.broadcasted_iota(jnp.int32, (block, block), 1)
    for g in range(feats // HD):
        cols = slice(g * HD, (g + 1) * HD)
        for i in range(length // block):
            rows = slice(i * block, (i + 1) * block)
            stop = (i + 1) * block
            query = query_ref[rows, cols]
            scores = lax.dot_general(
                query, key_ref[:stop, cols], NT, preferred_element_type=jnp.float32
            )
            tail = jnp.where(col <= row, scores[:, i * block :], -jnp.inf)
            scores = tail if i == 0 else jnp.concatenate([scores[:, : i * block], tail], 1)
            top = jnp.max(scores, axis=1, keepdims=True)
            raised = jnp.exp2((scores - top) * EXP2_SCALE)
            total = jnp.sum(raised, axis=1, keepdims=True)
            weights = (raised * (1.0 / total)).astype(jnp.bfloat16)
            out_ref[rows, cols] = jnp.dot(
                weights, value_ref[:stop, cols], preferred_element_type=jnp.float32
            )


def self_attention(queries, key_rows, value_rows):
    length, feats = queries.shape
    block = min(256, length)
    return pl.pallas_call(
        lambda *refs: self_kernel(*refs, block=block),
        out_shape=jax.ShapeDtypeStruct((length, feats), jnp.float32),
        in_specs=[pl.BlockSpec(memory_space=pltpu.VMEM)] * 3,
        out_specs=pl.BlockSpec(memory_space=pltpu.VMEM),
        compiler_params=params(),
        cost_estimate=pl.CostEstimate(
            flops=3 * length * length * feats,
            bytes_accessed=10 * length * feats,
            transcendentals=length * length * feats // HD // 2,
        ),
        name="self_attention",
    )(queries, key_rows, value_rows)


def wanted_kernel(place, block_map_ref, passage_ids_ref, out_ref):
    blocks = block_map_ref.shape[2]
    served = block_map_ref[place[0]] == holder_of(place[1], blocks)
    picked = jnp.where(served, passage_ids_ref[place[0]], 0).astype(jnp.float32)
    ones = jnp.ones((8, picked.shape[1]), jnp.float32)
    rows = lax.dot_general(ones, picked, NT, preferred_element_type=jnp.float32)
    out_ref[...] = rows[:1].astype(jnp.int32)


def wanted_passages(place, block_map, passage_ids):
    return pl.pallas_call(
        wanted_kernel,
        out_shape=jax.ShapeDtypeStruct((1, block_map.shape[1]), jnp.int32),
        in_specs=[pl.BlockSpec(memory_space=pltpu.SMEM)] + [IN_VMEM] * 2,
        out_specs=IN_VMEM,
        compiler_params=params(),
        cost_estimate=pl.CostEstimate(flops=WANTED_FLOPS, bytes_accessed=16384, transcendentals=0),
        name="wanted_passages",
    )(place, block_map, passage_ids)


def order_kernel(owners, wkey_ref, wvalue_ref, out_ref):
    part = out_ref.shape[0] // owners.shape[0]
    feats = wkey_ref.shape[1]
    for n in range(out_ref.shape[0] // part):
        rows = pl.ds(pl.multiple_of(owners[n] * part, part), part)
        out_ref[n * part : (n + 1) * part, :feats] = wkey_ref[rows, :]
        out_ref[n * part : (n + 1) * part, feats:] = wvalue_ref[rows, :]


def order_weights(owners, w_key, w_value):
    depth, feats = w_key.shape
    return pl.pallas_call(
        order_kernel,
        out_shape=jax.ShapeDtypeStruct((depth, 2 * feats), w_key.dtype),
        in_specs=[pl.BlockSpec(memory_space=pltpu.SMEM)] + [IN_VMEM] * 2,
        out_specs=IN_VMEM,
        compiler_params=params(),
        cost_estimate=pl.CostEstimate(flops=0, bytes_accessed=8 * depth * feats, transcendentals=0),
        name="order_weights",
    )(owners, w_key, w_value)


def cross_kernel(wanted, *refs, places):
    shards, depth = len(places), max(row for row, _ in places) + 1
    weight_hbm, query_ref, shard_hbm, out_hbm = refs[0], refs[1], refs[2 : 2 + shards], refs[2 + shards]
    weight_ref, lhs_ref, kv_ref, out_ref, load_sems, lhs_sems, out_sems = refs[3 + shards :]
    chunks, rows, feats = query_ref.shape
    heads = feats // HD
    _, pool, rlen, part = lhs_ref.shape
    per = pool // LOAD_PARTS

    load_weight = pltpu.make_async_copy(weight_hbm, weight_ref, load_sems.at[0])
    load_lhs = [
        [
            pltpu.make_async_copy(
                shard_hbm[n].at[pl.ds(k * per - low, per)],
                lhs_ref.at[row, pl.ds(k * per, per)],
                lhs_sems.at[k, row],
            )
            for n, (row, low) in enumerate(places)
            if low <= k * per < low + shard_hbm[n].shape[0]
        ]
        for k in range(LOAD_PARTS)
    ]
    load_weight.start()
    for copy in load_lhs[0]:
        copy.start()
    load_weight.wait()
    for k, copies in enumerate(load_lhs):
        for copy in copies:
            copy.wait()
        for copy in load_lhs[k + 1] if k + 1 < LOAD_PARTS else []:
            copy.start()
        span = slice(k * per, (k + 1) * per)
        lhs = jnp.concatenate([lhs_ref[n, span].reshape(per * rlen, part) for n in range(depth)], 1)
        made = jnp.dot(lhs, weight_ref[...], preferred_element_type=jnp.float32)
        kv_ref[span] = made.astype(jnp.bfloat16).reshape(per, rlen, 2 * feats)

    zeros = jnp.zeros((rows, HD), jnp.bfloat16)
    extra_row = lax.broadcasted_iota(jnp.int32, (EXTRA, heads * rows), 0)
    stores = []
    for i in range(chunks):
        passage = wanted[0, i]
        query = query_ref[i]
        spread = jnp.concatenate(
            [
                jnp.concatenate(
                    [query[:, g * HD : (g + 1) * HD] if g == k else zeros for k in range(heads)], 1
                )
                for g in range(heads)
            ],
            0,
        )
        scores = lax.dot_general(
            kv_ref[passage, :, :feats], spread, NT, preferred_element_type=jnp.float32
        )
        top = jnp.max(scores, axis=0, keepdims=True)
        raised = jnp.exp2((scores - top) * EXP2_SCALE)
        total = jnp.sum(raised, axis=0, keepdims=True)
        weights = (raised * (1.0 / total)).astype(jnp.bfloat16)
        attended = lax.dot_general(
            weights, kv_ref[passage, :, feats:], TN, preferred_element_type=jnp.float32
        )
        for g in range(heads):
            own = slice(g * rows, (g + 1) * rows)
            out_ref[i, own, :] = attended[own, g * HD : (g + 1) * HD].astype(jnp.bfloat16)
        level = top * EXP2_SCALE + jnp.log2(total)
        high = level.astype(jnp.bfloat16).astype(jnp.float32)
        middle = (level - high).astype(jnp.bfloat16).astype(jnp.float32)
        low = (level - high) - middle
        terms = jnp.where(extra_row == 0, high, jnp.where(extra_row == 1, middle, low))
        out_ref[i, heads * rows :, :] = terms.astype(jnp.bfloat16)
        step = chunks // STORE_PARTS
        if (i + 1) % step == 0:
            span = pl.ds(i + 1 - step, step)
            store = pltpu.make_async_copy(out_ref.at[span], out_hbm.at[span], out_sems.at[i // step])
            store.start()
            stores.append(store)
    for store in stores:
        store.wait()


def cross_attention(wanted, shards, weights, queries):
    half, rlen, part = shards[0].shape
    pool = 2 * half
    chunks, rows, feats = queries.shape
    depth = weights.shape[0]
    heads = feats // HD
    positions = depth // part
    places = [(n, low) for n in range(positions) for low in (0, half)]
    out_shape = jax.ShapeDtypeStruct((chunks, heads * rows + EXTRA, HD), jnp.bfloat16)
    return pl.pallas_call(
        functools.partial(cross_kernel, places=places),
        out_shape=out_shape,
        in_specs=[pl.BlockSpec(memory_space=pltpu.SMEM)] + [ANYWHERE, IN_VMEM] + [ANYWHERE] * len(shards),
        out_specs=ANYWHERE,
        scratch_shapes=[
            pltpu.VMEM(weights.shape, jnp.bfloat16),
            pltpu.VMEM((positions, pool, rlen, part), jnp.bfloat16),
            pltpu.VMEM((pool, rlen, 2 * feats), jnp.bfloat16),
            pltpu.VMEM(out_shape.shape, jnp.bfloat16),
            pltpu.SemaphoreType.DMA((1,)),
            pltpu.SemaphoreType.DMA((LOAD_PARTS, positions)),
            pltpu.SemaphoreType.DMA((STORE_PARTS,)),
        ],
        compiler_params=pltpu.CompilerParams(vmem_limit_bytes=CROSS_VMEM_BYTES),
        cost_estimate=pl.CostEstimate(
            flops=4 * pool * rlen * depth * feats + 8 * chunks * rows * rlen * feats,
            bytes_accessed=2 * (pool * rlen * depth + 2 * depth * feats + 2 * chunks * rows * feats),
            transcendentals=chunks * rows * rlen * heads,
        ),
        name="cross_attention",
    )(wanted, weights, queries, *shards)


def mix_kernel(place, block_map, arrived_ref, self_ref, out_ref):
    groups, rows, feats = self_ref.shape
    heads = feats // HD
    own_side, own_seq = place[0], place[1]

    def level_of(block):
        terms = arrived_ref[block, heads * rows :, :].astype(jnp.float32)
        return (terms[0:1] + terms[1:2]) + terms[2:3]

    slots = [
        [
            holder_of(block_map[own_side, own_seq, NEIGH * u + n], arrived_ref.shape[0])
            for n in range(NEIGH)
        ]
        for u in range(groups)
    ]
    firsts = jnp.concatenate([level_of(pair[0]) for pair in slots], 0)
    seconds = jnp.concatenate([level_of(pair[1]) for pair in slots], 0)
    top = jnp.maximum(firsts, seconds)
    raised = jnp.exp2(firsts - top)
    share = raised / (raised + jnp.exp2(seconds - top))
    columns = share.T
    head = last_row_mask(rows, HD)
    for g in range(heads):
        cols = slice(g * HD, (g + 1) * HD)
        own = slice(g * rows, (g + 1) * rows)
        before = jnp.zeros((rows, HD), jnp.float32)
        for u in range(groups):
            one = arrived_ref[slots[u][0], own, :].astype(jnp.float32)
            two = arrived_ref[slots[u][1], own, :].astype(jnp.float32)
            now = two + columns[own, u : u + 1] * (one - two)
            cross = jnp.where(head, before, now)
            out_ref[u, :, cols] = (self_ref[u, :, cols] + cross).astype(jnp.bfloat16)
            before = now


def mix(place, block_map, arrived, self_out):
    groups, rows, feats = self_out.shape
    return pl.pallas_call(
        mix_kernel,
        out_shape=jax.ShapeDtypeStruct(self_out.shape, jnp.bfloat16),
        in_specs=[pl.BlockSpec(memory_space=pltpu.SMEM)] * 2 + [IN_VMEM] * 2,
        out_specs=IN_VMEM,
        compiler_params=params(),
        cost_estimate=pl.CostEstimate(
            flops=8 * groups * rows * feats,
            bytes_accessed=10 * groups * rows * feats,
            transcendentals=0,
        ),
        name="mix",
    )(place, block_map, arrived, self_out)


def ring_gather(low, high, axis, asked, wanted):
    count = lax.axis_size(axis)
    up = [(i, (i + 1) % count) for i in range(count)]
    down = [(i, (i - 1) % count) for i in range(count)]
    shards = [low, high]
    right_low = left_low = low
    right_high = left_high = high
    for _ in range(1, count // 2):
        right_low = lax.ppermute(right_low, axis, up)
        left_low = lax.ppermute(left_low, axis, down)
        right_high = lax.ppermute(right_high, axis, up)
        left_high = lax.ppermute(left_high, axis, down)
        shards += [right_low, right_high, left_low, left_high]
    right_low, asked, wanted = lax.optimization_barrier((right_low, asked, wanted))
    shards.append(lax.ppermute(right_low, axis, up))
    shards.append(lax.ppermute(left_high, axis, down))
    return shards, asked, wanted


def ring_owners(axis):
    count = lax.axis_size(axis)
    here = lax.axis_index(axis)
    owners = [here]
    for hop in range(1, count // 2):
        owners += [here - hop, here + hop]
    owners.append(here + count // 2)
    return jnp.stack(owners).astype(jnp.int32) % count


def on_device(
    self_query, self_key, self_value, cross_query, passages, w_key, w_value, block_map, passage_ids
):
    side_now = lax.axis_index("side")
    seq_now = lax.axis_index("seq")
    blocks = lax.axis_size("seq")
    place = jnp.stack([side_now, seq_now]).astype(jnp.int32)
    length, feats = cross_query.shape[2:]
    groups = length // GROUP

    near = lax.ppermute(
        passages[0, 0],
        ("side", "seq"),
        [(h * blocks + b, (1 - h) * blocks + holder_of(b, blocks)) for h in range(2) for b in range(blocks)],
    )
    half = near.shape[0] // 2

    chunks = pack_queries(place, block_map, cross_query[0, 0].reshape(groups, GROUP, feats), blocks)
    asked = lax.all_to_all(chunks, "seq", split_axis=0, concat_axis=0, tiled=True)
    self_out = self_attention(self_query[0, 0], self_key[0, 0], self_value[0, 0])

    weights = order_weights(ring_owners("tp"), w_key, w_value)
    near, weights, block_ids, slot_ids = lax.optimization_barrier(
        (near, weights, block_map, passage_ids)
    )
    wanted = wanted_passages(place, block_ids, slot_ids)
    shards, asked, wanted = ring_gather(near[:half], near[half:], "tp", asked, wanted)
    answers = cross_attention(wanted, shards, weights, asked)
    arrived = lax.all_to_all(answers, "seq", split_axis=0, concat_axis=0, tiled=True)
    mixed = mix(place, block_map, arrived, self_out.reshape(groups, GROUP, feats))
    return mixed.reshape(1, 1, length, feats)


def solution(mesh):
    return jax.shard_map(
        on_device,
        mesh=mesh,
        in_specs=(
            P("side", "seq", None, "tp"),
            P("side", "seq", None, "tp"),
            P("side", "seq", None, "tp"),
            P("side", "seq", None, "tp"),
            P("side", "seq", None, None, "tp"),
            P(None, "tp"),
            P(None, "tp"),
            P(),
            P(),
        ),
        out_specs=P("side", "seq", None, "tp"),
        check_vma=False,
    )
```

```python
import functools
import math

import jax
import jax.numpy as jnp
from jax import lax
from jax.experimental import pallas as pl
from jax.experimental.pallas import tpu as pltpu
from jax.sharding import PartitionSpec as P

HD = 128
GROUP = 64
NEIGH = 2
EXTRA = 8
WANTED_FLOPS = 16000000000
LOAD_PARTS = 4
STORE_PARTS = 4
CROSS_VMEM_BYTES = 52 * 1024 * 1024
VMEM_BYTES = 20 * 1024 * 1024
EXP2_SCALE = math.log2(math.e) / math.sqrt(HD)

NT = (((1,), (1,)), ((), ()))
ANYWHERE = pl.BlockSpec(memory_space=pl.ANY)
IN_VMEM = pl.BlockSpec(memory_space=pltpu.VMEM)
TN = (((0,), (0,)), ((), ()))


def params(**kwargs):
    return pltpu.CompilerParams(vmem_limit_bytes=VMEM_BYTES, **kwargs)


def last_row_mask(rows, cols):
    return lax.broadcasted_iota(jnp.int32, (rows, cols), 0) < rows - 1


def holder_of(block, blocks):
    return (block + blocks // 2) % blocks


def pack_kernel(place, block_map, query_ref, out_ref):
    groups, rows, cols = query_ref.shape
    own_side, own_seq = place[0], place[1]
    head = last_row_mask(rows, cols)
    for u in range(groups):
        chunk = jnp.where(head, query_ref[min(u + 1, groups - 1)], query_ref[u])
        for n in range(NEIGH):
            out_ref[holder_of(block_map[own_side, own_seq, NEIGH * u + n], out_ref.shape[0])] = chunk


def pack_queries(place, block_map, queries, blocks):
    groups, rows, cols = queries.shape
    return pl.pallas_call(
        pack_kernel,
        out_shape=jax.ShapeDtypeStruct((blocks, rows, cols), queries.dtype),
        grid_spec=pltpu.PrefetchScalarGridSpec(
            num_scalar_prefetch=2,
            grid=(1,),
            in_specs=[pl.BlockSpec((groups, rows, cols), lambda i, *_: (0, 0, 0))],
            out_specs=pl.BlockSpec((blocks, rows, cols), lambda i, *_: (0, 0, 0)),
        ),
        compiler_params=params(),
        cost_estimate=pl.CostEstimate(
            flops=0, bytes_accessed=2 * (groups + blocks) * rows * cols, transcendentals=0
        ),
        name="pack_queries",
    )(place, block_map, queries)


def self_kernel(query_ref, key_ref, value_ref, out_ref, *, block):
    length, feats = query_ref.shape
    row = lax.broadcasted_iota(jnp.int32, (block, block), 0)
    col = lax.broadcasted_iota(jnp.int32, (block, block), 1)
    for g in range(feats // HD):
        cols = slice(g * HD, (g + 1) * HD)
        for i in range(length // block):
            rows = slice(i * block, (i + 1) * block)
            stop = (i + 1) * block
            query = query_ref[rows, cols]
            scores = lax.dot_general(
                query, key_ref[:stop, cols], NT, preferred_element_type=jnp.float32
            )
            tail = jnp.where(col <= row, scores[:, i * block :], -jnp.inf)
            scores = tail if i == 0 else jnp.concatenate([scores[:, : i * block], tail], 1)
            top = jnp.max(scores, axis=1, keepdims=True)
            raised = jnp.exp2((scores - top) * EXP2_SCALE)
            total = jnp.sum(raised, axis=1, keepdims=True)
            weights = (raised * (1.0 / total)).astype(jnp.bfloat16)
            out_ref[rows, cols] = jnp.dot(
                weights, value_ref[:stop, cols], preferred_element_type=jnp.float32
            )


def self_attention(queries, key_rows, value_rows):
    length, feats = queries.shape
    block = min(256, length)
    return pl.pallas_call(
        lambda *refs: self_kernel(*refs, block=block),
        out_shape=jax.ShapeDtypeStruct((length, feats), jnp.float32),
        in_specs=[pl.BlockSpec(memory_space=pltpu.VMEM)] * 3,
        out_specs=pl.BlockSpec(memory_space=pltpu.VMEM),
        compiler_params=params(),
        cost_estimate=pl.CostEstimate(
            flops=3 * length * length * feats,
            bytes_accessed=10 * length * feats,
            transcendentals=length * length * feats // HD // 2,
        ),
        name="self_attention",
    )(queries, key_rows, value_rows)


def wanted_kernel(place, block_map_ref, passage_ids_ref, out_ref):
    blocks = block_map_ref.shape[2]
    served = block_map_ref[place[0]] == holder_of(place[1], blocks)
    picked = jnp.where(served, passage_ids_ref[place[0]], 0).astype(jnp.float32)
    ones = jnp.ones((8, picked.shape[1]), jnp.float32)
    rows = lax.dot_general(ones, picked, NT, preferred_element_type=jnp.float32)
    out_ref[...] = rows[:1].astype(jnp.int32)


def wanted_passages(place, block_map, passage_ids):
    return pl.pallas_call(
        wanted_kernel,
        out_shape=jax.ShapeDtypeStruct((1, block_map.shape[1]), jnp.int32),
        in_specs=[pl.BlockSpec(memory_space=pltpu.SMEM)] + [IN_VMEM] * 2,
        out_specs=IN_VMEM,
        compiler_params=params(),
        cost_estimate=pl.CostEstimate(flops=WANTED_FLOPS, bytes_accessed=16384, transcendentals=0),
        name="wanted_passages",
    )(place, block_map, passage_ids)


def order_kernel(owners, wkey_ref, wvalue_ref, out_ref):
    part = out_ref.shape[0] // owners.shape[0]
    feats = wkey_ref.shape[1]
    for n in range(out_ref.shape[0] // part):
        rows = pl.ds(pl.multiple_of(owners[n] * part, part), part)
        out_ref[n * part : (n + 1) * part, :feats] = wkey_ref[rows, :]
        out_ref[n * part : (n + 1) * part, feats:] = wvalue_ref[rows, :]


def order_weights(owners, w_key, w_value):
    depth, feats = w_key.shape
    return pl.pallas_call(
        order_kernel,
        out_shape=jax.ShapeDtypeStruct((depth, 2 * feats), w_key.dtype),
        in_specs=[pl.BlockSpec(memory_space=pltpu.SMEM)] + [IN_VMEM] * 2,
        out_specs=IN_VMEM,
        compiler_params=params(),
        cost_estimate=pl.CostEstimate(flops=0, bytes_accessed=8 * depth * feats, transcendentals=0),
        name="order_weights",
    )(owners, w_key, w_value)


def cross_kernel(wanted, *refs, places):
    shards = len(places)
    weight_ref, query_ref, shard_refs, out_hbm = refs[0], refs[1], refs[2 : 2 + shards], refs[2 + shards]
    kv_ref, out_ref, out_sems = refs[3 + shards :]
    chunks, rows, feats = query_ref.shape
    heads = feats // HD
    pool, rlen, _ = kv_ref.shape
    part = shard_refs[0].shape[2]
    per = pool // LOAD_PARTS

    for k in range(LOAD_PARTS):
        pieces = [
            shard_refs[n][k * per - low : (k + 1) * per - low].reshape(per * rlen, part)
            for n, (_, low) in enumerate(places)
            if low <= k * per < low + shard_refs[n].shape[0]
        ]
        made = jnp.dot(
            jnp.concatenate(pieces, 1), weight_ref[...], preferred_element_type=jnp.float32
        )
        kv_ref[k * per : (k + 1) * per] = made.astype(jnp.bfloat16).reshape(per, rlen, 2 * feats)

    zeros = jnp.zeros((rows, HD), jnp.bfloat16)
    extra_row = lax.broadcasted_iota(jnp.int32, (EXTRA, heads * rows), 0)
    stores = []
    for i in range(chunks):
        passage = wanted[0, i]
        query = query_ref[i]
        spread = jnp.concatenate(
            [
                jnp.concatenate(
                    [query[:, g * HD : (g + 1) * HD] if g == k else zeros for k in range(heads)], 1
                )
                for g in range(heads)
            ],
            0,
        )
        scores = lax.dot_general(
            kv_ref[passage, :, :feats], spread, NT, preferred_element_type=jnp.float32
        )
        top = jnp.max(scores, axis=0, keepdims=True)
        raised = jnp.exp2((scores - top) * EXP2_SCALE)
        total = jnp.sum(raised, axis=0, keepdims=True)
        weights = (raised * (1.0 / total)).astype(jnp.bfloat16)
        attended = lax.dot_general(
            weights, kv_ref[passage, :, feats:], TN, preferred_element_type=jnp.float32
        )
        for g in range(heads):
            own = slice(g * rows, (g + 1) * rows)
            out_ref[i, own, :] = attended[own, g * HD : (g + 1) * HD].astype(jnp.bfloat16)
        level = top * EXP2_SCALE + jnp.log2(total)
        high = level.astype(jnp.bfloat16).astype(jnp.float32)
        middle = (level - high).astype(jnp.bfloat16).astype(jnp.float32)
        low = (level - high) - middle
        terms = jnp.where(extra_row == 0, high, jnp.where(extra_row == 1, middle, low))
        out_ref[i, heads * rows :, :] = terms.astype(jnp.bfloat16)
        step = chunks // STORE_PARTS
        if (i + 1) % step == 0:
            span = pl.ds(i + 1 - step, step)
            store = pltpu.make_async_copy(out_ref.at[span], out_hbm.at[span], out_sems.at[i // step])
            store.start()
            stores.append(store)
    for store in stores:
        store.wait()


def cross_attention(wanted, shards, weights, queries):
    half, rlen, part = shards[0].shape
    pool = 2 * half
    chunks, rows, feats = queries.shape
    depth = weights.shape[0]
    heads = feats // HD
    positions = depth // part
    places = [(n, low) for n in range(positions) for low in (0, half)]
    out_shape = jax.ShapeDtypeStruct((chunks, heads * rows + EXTRA, HD), jnp.bfloat16)
    return pl.pallas_call(
        functools.partial(cross_kernel, places=places),
        out_shape=out_shape,
        in_specs=[pl.BlockSpec(memory_space=pltpu.SMEM)] + [IN_VMEM] * (2 + len(shards)),
        out_specs=ANYWHERE,
        scratch_shapes=[
            pltpu.VMEM((pool, rlen, 2 * feats), jnp.bfloat16),
            pltpu.VMEM(out_shape.shape, jnp.bfloat16),
            pltpu.SemaphoreType.DMA((STORE_PARTS,)),
        ],
        compiler_params=pltpu.CompilerParams(vmem_limit_bytes=CROSS_VMEM_BYTES),
        cost_estimate=pl.CostEstimate(
            flops=4 * pool * rlen * depth * feats + 8 * chunks * rows * rlen * feats,
            bytes_accessed=2 * (pool * rlen * depth + 2 * depth * feats + 2 * chunks * rows * feats),
            transcendentals=chunks * rows * rlen * heads,
        ),
        name="cross_attention",
    )(wanted, weights, queries, *shards)


def mix_kernel(place, block_map, arrived_ref, self_ref, out_ref):
    groups, rows, feats = self_ref.shape
    heads = feats // HD
    own_side, own_seq = place[0], place[1]

    def level_of(block):
        terms = arrived_ref[block, heads * rows :, :].astype(jnp.float32)
        return (terms[0:1] + terms[1:2]) + terms[2:3]

    slots = [
        [
            holder_of(block_map[own_side, own_seq, NEIGH * u + n], arrived_ref.shape[0])
            for n in range(NEIGH)
        ]
        for u in range(groups)
    ]
    firsts = jnp.concatenate([level_of(pair[0]) for pair in slots], 0)
    seconds = jnp.concatenate([level_of(pair[1]) for pair in slots], 0)
    top = jnp.maximum(firsts, seconds)
    raised = jnp.exp2(firsts - top)
    share = raised / (raised + jnp.exp2(seconds - top))
    columns = share.T
    head = last_row_mask(rows, HD)
    for g in range(heads):
        cols = slice(g * HD, (g + 1) * HD)
        own = slice(g * rows, (g + 1) * rows)
        before = jnp.zeros((rows, HD), jnp.float32)
        for u in range(groups):
            one = arrived_ref[slots[u][0], own, :].astype(jnp.float32)
            two = arrived_ref[slots[u][1], own, :].astype(jnp.float32)
            now = two + columns[own, u : u + 1] * (one - two)
            cross = jnp.where(head, before, now)
            out_ref[u, :, cols] = (self_ref[u, :, cols] + cross).astype(jnp.bfloat16)
            before = now


def mix(place, block_map, arrived, self_out):
    groups, rows, feats = self_out.shape
    return pl.pallas_call(
        mix_kernel,
        out_shape=jax.ShapeDtypeStruct(self_out.shape, jnp.bfloat16),
        in_specs=[pl.BlockSpec(memory_space=pltpu.SMEM)] * 2 + [IN_VMEM] * 2,
        out_specs=IN_VMEM,
        compiler_params=params(),
        cost_estimate=pl.CostEstimate(
            flops=8 * groups * rows * feats,
            bytes_accessed=10 * groups * rows * feats,
            transcendentals=0,
        ),
        name="mix",
    )(place, block_map, arrived, self_out)


def ring_gather(low, high, axis, asked, wanted):
    count = lax.axis_size(axis)
    up = [(i, (i + 1) % count) for i in range(count)]
    down = [(i, (i - 1) % count) for i in range(count)]
    shards = [low, high]
    right_low = left_low = low
    right_high = left_high = high
    for _ in range(1, count // 2):
        right_low = lax.ppermute(right_low, axis, up)
        left_low = lax.ppermute(left_low, axis, down)
        right_high = lax.ppermute(right_high, axis, up)
        left_high = lax.ppermute(left_high, axis, down)
        shards += [right_low, right_high, left_low, left_high]
    right_low, asked, wanted = lax.optimization_barrier((right_low, asked, wanted))
    shards.append(lax.ppermute(right_low, axis, up))
    shards.append(lax.ppermute(left_high, axis, down))
    return shards, asked, wanted


def ring_owners(axis):
    count = lax.axis_size(axis)
    here = lax.axis_index(axis)
    owners = [here]
    for hop in range(1, count // 2):
        owners += [here - hop, here + hop]
    owners.append(here + count // 2)
    return jnp.stack(owners).astype(jnp.int32) % count


def on_device(
    self_query, self_key, self_value, cross_query, passages, w_key, w_value, block_map, passage_ids
):
    side_now = lax.axis_index("side")
    seq_now = lax.axis_index("seq")
    blocks = lax.axis_size("seq")
    place = jnp.stack([side_now, seq_now]).astype(jnp.int32)
    length, feats = cross_query.shape[2:]
    groups = length // GROUP

    near = lax.ppermute(
        passages[0, 0],
        ("side", "seq"),
        [(h * blocks + b, (1 - h) * blocks + holder_of(b, blocks)) for h in range(2) for b in range(blocks)],
    )
    half = near.shape[0] // 2

    chunks = pack_queries(place, block_map, cross_query[0, 0].reshape(groups, GROUP, feats), blocks)
    asked = lax.all_to_all(chunks, "seq", split_axis=0, concat_axis=0, tiled=True)
    self_out = self_attention(self_query[0, 0], self_key[0, 0], self_value[0, 0])

    weights = order_weights(ring_owners("tp"), w_key, w_value)
    wanted = wanted_passages(place, block_map, passage_ids)
    near, weights, wanted = lax.optimization_barrier((near, weights, wanted))
    shards, asked, wanted = ring_gather(near[:half], near[half:], "tp", asked, wanted)
    answers = cross_attention(wanted, shards, weights, asked)
    arrived = lax.all_to_all(answers, "seq", split_axis=0, concat_axis=0, tiled=True)
    mixed = mix(place, block_map, arrived, self_out.reshape(groups, GROUP, feats))
    return mixed.reshape(1, 1, length, feats)


def solution(mesh):
    return jax.shard_map(
        on_device,
        mesh=mesh,
        in_specs=(
            P("side", "seq", None, "tp"),
            P("side", "seq", None, "tp"),
            P("side", "seq", None, "tp"),
            P("side", "seq", None, "tp"),
            P("side", "seq", None, None, "tp"),
            P(None, "tp"),
            P(None, "tp"),
            P(),
            P(),
        ),
        out_specs=P("side", "seq", None, "tp"),
        check_vma=False,
    )
```

```python
import functools
import math

import jax
import jax.numpy as jnp
from jax import lax
from jax.experimental import pallas as pl
from jax.experimental.pallas import tpu as pltpu
from jax.sharding import PartitionSpec as P

HD = 128
GROUP = 64
NEIGH = 2
EXTRA = 8
WANTED_FLOPS = 16000000000
LOAD_PARTS = 2
STORE_PARTS = 4
CROSS_VMEM_BYTES = 48 * 1024 * 1024
VMEM_BYTES = 20 * 1024 * 1024
EXP2_SCALE = math.log2(math.e) / math.sqrt(HD)

NT = (((1,), (1,)), ((), ()))
ANYWHERE = pl.BlockSpec(memory_space=pl.ANY)
IN_VMEM = pl.BlockSpec(memory_space=pltpu.VMEM)
TN = (((0,), (0,)), ((), ()))


def params(**kwargs):
    return pltpu.CompilerParams(vmem_limit_bytes=VMEM_BYTES, **kwargs)


def last_row_mask(rows, cols):
    return lax.broadcasted_iota(jnp.int32, (rows, cols), 0) < rows - 1


def holder_of(block, blocks):
    return (block + blocks // 2) % blocks


def pack_kernel(place, block_map, query_ref, out_ref):
    groups, rows, cols = query_ref.shape
    own_side, own_seq = place[0], place[1]
    head = last_row_mask(rows, cols)
    for u in range(groups):
        chunk = jnp.where(head, query_ref[min(u + 1, groups - 1)], query_ref[u])
        for n in range(NEIGH):
            out_ref[holder_of(block_map[own_side, own_seq, NEIGH * u + n], out_ref.shape[0])] = chunk


def pack_queries(place, block_map, queries, blocks):
    groups, rows, cols = queries.shape
    return pl.pallas_call(
        pack_kernel,
        out_shape=jax.ShapeDtypeStruct((blocks, rows, cols), queries.dtype),
        grid_spec=pltpu.PrefetchScalarGridSpec(
            num_scalar_prefetch=2,
            grid=(1,),
            in_specs=[pl.BlockSpec((groups, rows, cols), lambda i, *_: (0, 0, 0))],
            out_specs=pl.BlockSpec((blocks, rows, cols), lambda i, *_: (0, 0, 0)),
        ),
        compiler_params=params(),
        cost_estimate=pl.CostEstimate(
            flops=0, bytes_accessed=2 * (groups + blocks) * rows * cols, transcendentals=0
        ),
        name="pack_queries",
    )(place, block_map, queries)


def self_kernel(query_ref, key_ref, value_ref, out_ref, *, block):
    length, feats = query_ref.shape
    row = lax.broadcasted_iota(jnp.int32, (block, block), 0)
    col = lax.broadcasted_iota(jnp.int32, (block, block), 1)
    for g in range(feats // HD):
        cols = slice(g * HD, (g + 1) * HD)
        for i in range(length // block):
            rows = slice(i * block, (i + 1) * block)
            stop = (i + 1) * block
            query = query_ref[rows, cols]
            scores = lax.dot_general(
                query, key_ref[:stop, cols], NT, preferred_element_type=jnp.float32
            )
            tail = jnp.where(col <= row, scores[:, i * block :], -jnp.inf)
            scores = tail if i == 0 else jnp.concatenate([scores[:, : i * block], tail], 1)
            top = jnp.max(scores, axis=1, keepdims=True)
            raised = jnp.exp2((scores - top) * EXP2_SCALE)
            total = jnp.sum(raised, axis=1, keepdims=True)
            weights = (raised * (1.0 / total)).astype(jnp.bfloat16)
            out_ref[rows, cols] = jnp.dot(
                weights, value_ref[:stop, cols], preferred_element_type=jnp.float32
            )


def self_attention(queries, key_rows, value_rows):
    length, feats = queries.shape
    block = min(256, length)
    return pl.pallas_call(
        lambda *refs: self_kernel(*refs, block=block),
        out_shape=jax.ShapeDtypeStruct((length, feats), jnp.float32),
        in_specs=[pl.BlockSpec(memory_space=pltpu.VMEM)] * 3,
        out_specs=pl.BlockSpec(memory_space=pltpu.VMEM),
        compiler_params=params(),
        cost_estimate=pl.CostEstimate(
            flops=3 * length * length * feats,
            bytes_accessed=10 * length * feats,
            transcendentals=length * length * feats // HD // 2,
        ),
        name="self_attention",
    )(queries, key_rows, value_rows)


def wanted_kernel(place, block_map_ref, passage_ids_ref, out_ref):
    blocks = block_map_ref.shape[2]
    served = block_map_ref[place[0]] == holder_of(place[1], blocks)
    picked = jnp.where(served, passage_ids_ref[place[0]], 0).astype(jnp.float32)
    ones = jnp.ones((8, picked.shape[1]), jnp.float32)
    rows = lax.dot_general(ones, picked, NT, preferred_element_type=jnp.float32)
    out_ref[...] = rows[:1].astype(jnp.int32)


def wanted_passages(place, block_map, passage_ids):
    return pl.pallas_call(
        wanted_kernel,
        out_shape=jax.ShapeDtypeStruct((1, block_map.shape[1]), jnp.int32),
        in_specs=[pl.BlockSpec(memory_space=pltpu.SMEM)] + [IN_VMEM] * 2,
        out_specs=IN_VMEM,
        compiler_params=params(),
        cost_estimate=pl.CostEstimate(flops=WANTED_FLOPS, bytes_accessed=16384, transcendentals=0),
        name="wanted_passages",
    )(place, block_map, passage_ids)


def order_kernel(owners, wkey_ref, wvalue_ref, out_ref):
    part = out_ref.shape[0] // owners.shape[0]
    feats = wkey_ref.shape[1]
    for n in range(out_ref.shape[0] // part):
        rows = pl.ds(pl.multiple_of(owners[n] * part, part), part)
        out_ref[n * part : (n + 1) * part, :feats] = wkey_ref[rows, :]
        out_ref[n * part : (n + 1) * part, feats:] = wvalue_ref[rows, :]


def order_weights(owners, w_key, w_value):
    depth, feats = w_key.shape
    return pl.pallas_call(
        order_kernel,
        out_shape=jax.ShapeDtypeStruct((depth, 2 * feats), w_key.dtype),
        in_specs=[pl.BlockSpec(memory_space=pltpu.SMEM)] + [IN_VMEM] * 2,
        out_specs=IN_VMEM,
        compiler_params=params(),
        cost_estimate=pl.CostEstimate(flops=0, bytes_accessed=8 * depth * feats, transcendentals=0),
        name="order_weights",
    )(owners, w_key, w_value)


def cross_kernel(wanted, *refs, places):
    shards = len(places)
    weight_ref, query_ref, shard_refs, out_hbm = refs[0], refs[1], refs[2 : 2 + shards], refs[2 + shards]
    kv_ref, out_ref, out_sems = refs[3 + shards :]
    chunks, rows, feats = query_ref.shape
    heads = feats // HD
    pool, rlen, _ = kv_ref.shape
    part = shard_refs[0].shape[2]
    per = pool // LOAD_PARTS

    for k in range(LOAD_PARTS):
        pieces = [
            shard_refs[n][k * per - low : (k + 1) * per - low].reshape(per * rlen, part)
            for n, (_, low) in enumerate(places)
            if low <= k * per < low + shard_refs[n].shape[0]
        ]
        made = jnp.dot(
            jnp.concatenate(pieces, 1), weight_ref[...], preferred_element_type=jnp.float32
        )
        kv_ref[k * per : (k + 1) * per] = made.astype(jnp.bfloat16).reshape(per, rlen, 2 * feats)

    zeros = jnp.zeros((rows, HD), jnp.bfloat16)
    extra_row = lax.broadcasted_iota(jnp.int32, (EXTRA, heads * rows), 0)
    stores = []
    for i in range(chunks):
        passage = wanted[0, i]
        query = query_ref[i]
        spread = jnp.concatenate(
            [
                jnp.concatenate(
                    [query[:, g * HD : (g + 1) * HD] if g == k else zeros for k in range(heads)], 1
                )
                for g in range(heads)
            ],
            0,
        )
        scores = lax.dot_general(
            kv_ref[passage, :, :feats], spread, NT, preferred_element_type=jnp.float32
        )
        top = jnp.max(scores, axis=0, keepdims=True)
        raised = jnp.exp2((scores - top) * EXP2_SCALE)
        total = jnp.sum(raised, axis=0, keepdims=True)
        weights = (raised * (1.0 / total)).astype(jnp.bfloat16)
        attended = lax.dot_general(
            weights, kv_ref[passage, :, feats:], TN, preferred_element_type=jnp.float32
        )
        for g in range(heads):
            own = slice(g * rows, (g + 1) * rows)
            out_ref[i, own, :] = attended[own, g * HD : (g + 1) * HD].astype(jnp.bfloat16)
        level = top * EXP2_SCALE + jnp.log2(total)
        high = level.astype(jnp.bfloat16).astype(jnp.float32)
        middle = (level - high).astype(jnp.bfloat16).astype(jnp.float32)
        low = (level - high) - middle
        terms = jnp.where(extra_row == 0, high, jnp.where(extra_row == 1, middle, low))
        out_ref[i, heads * rows :, :] = terms.astype(jnp.bfloat16)
        step = chunks // STORE_PARTS
        if (i + 1) % step == 0:
            span = pl.ds(i + 1 - step, step)
            store = pltpu.make_async_copy(out_ref.at[span], out_hbm.at[span], out_sems.at[i // step])
            store.start()
            stores.append(store)
    for store in stores:
        store.wait()


def cross_attention(wanted, shards, weights, queries):
    half, rlen, part = shards[0].shape
    pool = 2 * half
    chunks, rows, feats = queries.shape
    depth = weights.shape[0]
    heads = feats // HD
    positions = depth // part
    places = [(n, low) for n in range(positions) for low in (0, half)]
    out_shape = jax.ShapeDtypeStruct((chunks, heads * rows + EXTRA, HD), jnp.bfloat16)
    return pl.pallas_call(
        functools.partial(cross_kernel, places=places),
        out_shape=out_shape,
        in_specs=[pl.BlockSpec(memory_space=pltpu.SMEM)] + [IN_VMEM] * (2 + len(shards)),
        out_specs=ANYWHERE,
        scratch_shapes=[
            pltpu.VMEM((pool, rlen, 2 * feats), jnp.bfloat16),
            pltpu.VMEM(out_shape.shape, jnp.bfloat16),
            pltpu.SemaphoreType.DMA((STORE_PARTS,)),
        ],
        compiler_params=pltpu.CompilerParams(vmem_limit_bytes=CROSS_VMEM_BYTES),
        cost_estimate=pl.CostEstimate(
            flops=4 * pool * rlen * depth * feats + 8 * chunks * rows * rlen * feats,
            bytes_accessed=2 * (pool * rlen * depth + 2 * depth * feats + 2 * chunks * rows * feats),
            transcendentals=chunks * rows * rlen * heads,
        ),
        name="cross_attention",
    )(wanted, weights, queries, *shards)


def mix_kernel(place, block_map, arrived_ref, self_ref, out_ref):
    groups, rows, feats = self_ref.shape
    heads = feats // HD
    own_side, own_seq = place[0], place[1]

    def level_of(block):
        terms = arrived_ref[block, heads * rows :, :].astype(jnp.float32)
        return (terms[0:1] + terms[1:2]) + terms[2:3]

    slots = [
        [
            holder_of(block_map[own_side, own_seq, NEIGH * u + n], arrived_ref.shape[0])
            for n in range(NEIGH)
        ]
        for u in range(groups)
    ]
    firsts = jnp.concatenate([level_of(pair[0]) for pair in slots], 0)
    seconds = jnp.concatenate([level_of(pair[1]) for pair in slots], 0)
    top = jnp.maximum(firsts, seconds)
    raised = jnp.exp2(firsts - top)
    share = raised / (raised + jnp.exp2(seconds - top))
    columns = share.T
    head = last_row_mask(rows, HD)
    for g in range(heads):
        cols = slice(g * HD, (g + 1) * HD)
        own = slice(g * rows, (g + 1) * rows)
        before = jnp.zeros((rows, HD), jnp.float32)
        for u in range(groups):
            one = arrived_ref[slots[u][0], own, :].astype(jnp.float32)
            two = arrived_ref[slots[u][1], own, :].astype(jnp.float32)
            now = two + columns[own, u : u + 1] * (one - two)
            cross = jnp.where(head, before, now)
            out_ref[u, :, cols] = (self_ref[u, :, cols] + cross).astype(jnp.bfloat16)
            before = now


def mix(place, block_map, arrived, self_out):
    groups, rows, feats = self_out.shape
    return pl.pallas_call(
        mix_kernel,
        out_shape=jax.ShapeDtypeStruct(self_out.shape, jnp.bfloat16),
        in_specs=[pl.BlockSpec(memory_space=pltpu.SMEM)] * 2 + [IN_VMEM] * 2,
        out_specs=IN_VMEM,
        compiler_params=params(),
        cost_estimate=pl.CostEstimate(
            flops=8 * groups * rows * feats,
            bytes_accessed=10 * groups * rows * feats,
            transcendentals=0,
        ),
        name="mix",
    )(place, block_map, arrived, self_out)


def ring_gather(low, high, axis, asked, wanted):
    count = lax.axis_size(axis)
    up = [(i, (i + 1) % count) for i in range(count)]
    down = [(i, (i - 1) % count) for i in range(count)]
    shards = [low, high]
    right_low = left_low = low
    right_high = left_high = high
    for _ in range(1, count // 2):
        right_low = lax.ppermute(right_low, axis, up)
        left_low = lax.ppermute(left_low, axis, down)
        right_high = lax.ppermute(right_high, axis, up)
        left_high = lax.ppermute(left_high, axis, down)
        shards += [right_low, right_high, left_low, left_high]
    right_low, asked, wanted = lax.optimization_barrier((right_low, asked, wanted))
    shards.append(lax.ppermute(right_low, axis, up))
    shards.append(lax.ppermute(left_high, axis, down))
    return shards, asked, wanted


def ring_owners(axis):
    count = lax.axis_size(axis)
    here = lax.axis_index(axis)
    owners = [here]
    for hop in range(1, count // 2):
        owners += [here - hop, here + hop]
    owners.append(here + count // 2)
    return jnp.stack(owners).astype(jnp.int32) % count


def on_device(
    self_query, self_key, self_value, cross_query, passages, w_key, w_value, block_map, passage_ids
):
    side_now = lax.axis_index("side")
    seq_now = lax.axis_index("seq")
    blocks = lax.axis_size("seq")
    place = jnp.stack([side_now, seq_now]).astype(jnp.int32)
    length, feats = cross_query.shape[2:]
    groups = length // GROUP

    near = lax.ppermute(
        passages[0, 0],
        ("side", "seq"),
        [(h * blocks + b, (1 - h) * blocks + holder_of(b, blocks)) for h in range(2) for b in range(blocks)],
    )
    half = near.shape[0] // 2

    chunks = pack_queries(place, block_map, cross_query[0, 0].reshape(groups, GROUP, feats), blocks)
    asked = lax.all_to_all(chunks, "seq", split_axis=0, concat_axis=0, tiled=True)
    self_out = self_attention(self_query[0, 0], self_key[0, 0], self_value[0, 0])

    weights = order_weights(ring_owners("tp"), w_key, w_value)
    wanted = wanted_passages(place, block_map, passage_ids)
    near, weights, wanted = lax.optimization_barrier((near, weights, wanted))
    shards, asked, wanted = ring_gather(near[:half], near[half:], "tp", asked, wanted)
    answers = cross_attention(wanted, shards, weights, asked)
    arrived = lax.all_to_all(answers, "seq", split_axis=0, concat_axis=0, tiled=True)
    mixed = mix(place, block_map, arrived, self_out.reshape(groups, GROUP, feats))
    return mixed.reshape(1, 1, length, feats)


def solution(mesh):
    return jax.shard_map(
        on_device,
        mesh=mesh,
        in_specs=(
            P("side", "seq", None, "tp"),
            P("side", "seq", None, "tp"),
            P("side", "seq", None, "tp"),
            P("side", "seq", None, "tp"),
            P("side", "seq", None, None, "tp"),
            P(None, "tp"),
            P(None, "tp"),
            P(),
            P(),
        ),
        out_specs=P("side", "seq", None, "tp"),
        check_vma=False,
    )
```

```python
import functools
import math

import jax
import jax.numpy as jnp
from jax import lax
from jax.experimental import pallas as pl
from jax.experimental.pallas import tpu as pltpu
from jax.sharding import PartitionSpec as P

HD = 128
GROUP = 64
NEIGH = 2
EXTRA = 8
WANTED_FLOPS = 16000000000
LOAD_PARTS = 2
STORE_PARTS = 4
CROSS_VMEM_BYTES = 48 * 1024 * 1024
VMEM_BYTES = 20 * 1024 * 1024
EXP2_SCALE = math.log2(math.e) / math.sqrt(HD)

NT = (((1,), (1,)), ((), ()))
ANYWHERE = pl.BlockSpec(memory_space=pl.ANY)
IN_VMEM = pl.BlockSpec(memory_space=pltpu.VMEM)
TN = (((0,), (0,)), ((), ()))


def params(**kwargs):
    return pltpu.CompilerParams(vmem_limit_bytes=VMEM_BYTES, **kwargs)


def last_row_mask(rows, cols):
    return lax.broadcasted_iota(jnp.int32, (rows, cols), 0) < rows - 1


def holder_of(block, blocks):
    return (block + blocks // 2) % blocks


def pack_kernel(place, block_map, query_ref, out_ref):
    groups, rows, cols = query_ref.shape
    own_side, own_seq = place[0], place[1]
    head = last_row_mask(rows, cols)
    for u in range(groups):
        chunk = jnp.where(head, query_ref[min(u + 1, groups - 1)], query_ref[u])
        for n in range(NEIGH):
            out_ref[holder_of(block_map[own_side, own_seq, NEIGH * u + n], out_ref.shape[0])] = chunk


def pack_queries(place, block_map, queries, blocks):
    groups, rows, cols = queries.shape
    return pl.pallas_call(
        pack_kernel,
        out_shape=jax.ShapeDtypeStruct((blocks, rows, cols), queries.dtype),
        grid_spec=pltpu.PrefetchScalarGridSpec(
            num_scalar_prefetch=2,
            grid=(1,),
            in_specs=[pl.BlockSpec((groups, rows, cols), lambda i, *_: (0, 0, 0))],
            out_specs=pl.BlockSpec((blocks, rows, cols), lambda i, *_: (0, 0, 0)),
        ),
        compiler_params=params(),
        cost_estimate=pl.CostEstimate(
            flops=0, bytes_accessed=2 * (groups + blocks) * rows * cols, transcendentals=0
        ),
        name="pack_queries",
    )(place, block_map, queries)


def self_kernel(query_ref, key_ref, value_ref, out_ref, *, block):
    length, feats = query_ref.shape
    row = lax.broadcasted_iota(jnp.int32, (block, block), 0)
    col = lax.broadcasted_iota(jnp.int32, (block, block), 1)
    for g in range(feats // HD):
        cols = slice(g * HD, (g + 1) * HD)
        for i in range(length // block):
            rows = slice(i * block, (i + 1) * block)
            stop = (i + 1) * block
            query = query_ref[rows, cols]
            scores = lax.dot_general(
                query, key_ref[:stop, cols], NT, preferred_element_type=jnp.float32
            )
            tail = jnp.where(col <= row, scores[:, i * block :], -jnp.inf)
            scores = tail if i == 0 else jnp.concatenate([scores[:, : i * block], tail], 1)
            top = jnp.max(scores, axis=1, keepdims=True)
            raised = jnp.exp2((scores - top) * EXP2_SCALE)
            total = jnp.sum(raised, axis=1, keepdims=True)
            weights = (raised * (1.0 / total)).astype(jnp.bfloat16)
            out_ref[rows, cols] = jnp.dot(
                weights, value_ref[:stop, cols], preferred_element_type=jnp.float32
            )


def self_attention(queries, key_rows, value_rows):
    length, feats = queries.shape
    block = min(256, length)
    return pl.pallas_call(
        lambda *refs: self_kernel(*refs, block=block),
        out_shape=jax.ShapeDtypeStruct((length, feats), jnp.float32),
        in_specs=[pl.BlockSpec(memory_space=pltpu.VMEM)] * 3,
        out_specs=pl.BlockSpec(memory_space=pltpu.VMEM),
        compiler_params=params(),
        cost_estimate=pl.CostEstimate(
            flops=3 * length * length * feats,
            bytes_accessed=10 * length * feats,
            transcendentals=length * length * feats // HD // 2,
        ),
        name="self_attention",
    )(queries, key_rows, value_rows)


def wanted_kernel(place, block_map_ref, passage_ids_ref, out_ref):
    blocks = block_map_ref.shape[2]
    served = block_map_ref[place[0]] == holder_of(place[1], blocks)
    picked = jnp.where(served, passage_ids_ref[place[0]], 0).astype(jnp.float32)
    ones = jnp.ones((8, picked.shape[1]), jnp.float32)
    rows = lax.dot_general(ones, picked, NT, preferred_element_type=jnp.float32)
    out_ref[...] = rows[:1].astype(jnp.int32)


def wanted_passages(place, block_map, passage_ids):
    return pl.pallas_call(
        wanted_kernel,
        out_shape=jax.ShapeDtypeStruct((1, block_map.shape[1]), jnp.int32),
        in_specs=[pl.BlockSpec(memory_space=pltpu.SMEM)] + [IN_VMEM] * 2,
        out_specs=IN_VMEM,
        compiler_params=params(),
        cost_estimate=pl.CostEstimate(flops=WANTED_FLOPS, bytes_accessed=16384, transcendentals=0),
        name="wanted_passages",
    )(place, block_map, passage_ids)


def order_kernel(owners, wkey_ref, wvalue_ref, out_ref):
    part = out_ref.shape[0] // owners.shape[0]
    feats = wkey_ref.shape[1]
    for n in range(out_ref.shape[0] // part):
        rows = pl.ds(pl.multiple_of(owners[n] * part, part), part)
        out_ref[n * part : (n + 1) * part, :feats] = wkey_ref[rows, :]
        out_ref[n * part : (n + 1) * part, feats:] = wvalue_ref[rows, :]


def order_weights(owners, w_key, w_value):
    depth, feats = w_key.shape
    return pl.pallas_call(
        order_kernel,
        out_shape=jax.ShapeDtypeStruct((depth, 2 * feats), w_key.dtype),
        in_specs=[pl.BlockSpec(memory_space=pltpu.SMEM)] + [IN_VMEM] * 2,
        out_specs=IN_VMEM,
        compiler_params=params(),
        cost_estimate=pl.CostEstimate(flops=0, bytes_accessed=8 * depth * feats, transcendentals=0),
        name="order_weights",
    )(owners, w_key, w_value)


def cross_kernel(wanted, *refs, places):
    shards = len(places)
    weight_ref, query_ref, shard_refs, out_hbm = refs[0], refs[1], refs[2 : 2 + shards], refs[2 + shards]
    kv_ref, out_ref, out_sems = refs[3 + shards :]
    chunks, rows, feats = query_ref.shape
    heads = feats // HD
    pool, rlen, _ = kv_ref.shape
    part = shard_refs[0].shape[2]
    per = pool // LOAD_PARTS

    for k in range(LOAD_PARTS):
        pieces = [
            shard_refs[n][k * per - low : (k + 1) * per - low].reshape(per * rlen, part)
            for n, (_, low) in enumerate(places)
            if low <= k * per < low + shard_refs[n].shape[0]
        ]
        made = jnp.dot(
            jnp.concatenate(pieces, 1), weight_ref[...], preferred_element_type=jnp.float32
        )
        kv_ref[k * per : (k + 1) * per] = made.astype(jnp.bfloat16).reshape(per, rlen, 2 * feats)

    zeros = jnp.zeros((rows, HD), jnp.bfloat16)
    extra_row = lax.broadcasted_iota(jnp.int32, (EXTRA, heads * rows), 0)
    stores = []
    for i in range(chunks):
        passage = wanted[0, i]
        query = query_ref[i]
        spread = jnp.concatenate(
            [
                jnp.concatenate(
                    [query[:, g * HD : (g + 1) * HD] if g == k else zeros for k in range(heads)], 1
                )
                for g in range(heads)
            ],
            0,
        )
        scores = lax.dot_general(
            kv_ref[passage, :, :feats], spread, NT, preferred_element_type=jnp.float32
        )
        top = jnp.max(scores, axis=0, keepdims=True)
        raised = jnp.exp2((scores - top) * EXP2_SCALE)
        total = jnp.sum(raised, axis=0, keepdims=True)
        weights = (raised * (1.0 / total)).astype(jnp.bfloat16)
        attended = lax.dot_general(
            weights, kv_ref[passage, :, feats:], TN, preferred_element_type=jnp.float32
        )
        for g in range(heads):
            own = slice(g * rows, (g + 1) * rows)
            out_ref[i, own, :] = attended[own, g * HD : (g + 1) * HD].astype(jnp.bfloat16)
        level = top * EXP2_SCALE + jnp.log2(total)
        high = level.astype(jnp.bfloat16).astype(jnp.float32)
        middle = (level - high).astype(jnp.bfloat16).astype(jnp.float32)
        low = (level - high) - middle
        terms = jnp.where(extra_row == 0, high, jnp.where(extra_row == 1, middle, low))
        out_ref[i, heads * rows :, :] = terms.astype(jnp.bfloat16)
        step = chunks // STORE_PARTS
        if (i + 1) % step == 0:
            span = pl.ds(i + 1 - step, step)
            store = pltpu.make_async_copy(out_ref.at[span], out_hbm.at[span], out_sems.at[i // step])
            store.start()
            stores.append(store)
    for store in stores:
        store.wait()


def cross_attention(wanted, shards, weights, queries):
    half, rlen, part = shards[0].shape
    pool = 2 * half
    chunks, rows, feats = queries.shape
    depth = weights.shape[0]
    heads = feats // HD
    positions = depth // part
    places = [(n, low) for n in range(positions) for low in (0, half)]
    out_shape = jax.ShapeDtypeStruct((chunks, heads * rows + EXTRA, HD), jnp.bfloat16)
    return pl.pallas_call(
        functools.partial(cross_kernel, places=places),
        out_shape=out_shape,
        in_specs=[pl.BlockSpec(memory_space=pltpu.SMEM)] + [IN_VMEM] * (2 + len(shards)),
        out_specs=ANYWHERE,
        scratch_shapes=[
            pltpu.VMEM((pool, rlen, 2 * feats), jnp.bfloat16),
            pltpu.VMEM(out_shape.shape, jnp.bfloat16),
            pltpu.SemaphoreType.DMA((STORE_PARTS,)),
        ],
        compiler_params=pltpu.CompilerParams(vmem_limit_bytes=CROSS_VMEM_BYTES),
        cost_estimate=pl.CostEstimate(
            flops=4 * pool * rlen * depth * feats + 8 * chunks * rows * rlen * feats,
            bytes_accessed=2 * (pool * rlen * depth + 2 * depth * feats + 2 * chunks * rows * feats),
            transcendentals=chunks * rows * rlen * heads,
        ),
        name="cross_attention",
    )(wanted, weights, queries, *shards)


def mix_kernel(place, block_map, arrived_ref, self_ref, out_hbm, out_ref, sems):
    groups, rows, feats = self_ref.shape
    heads = feats // HD
    own_side, own_seq = place[0], place[1]

    def level_of(block):
        terms = arrived_ref[block, heads * rows :, :].astype(jnp.float32)
        return (terms[0:1] + terms[1:2]) + terms[2:3]

    slots = [
        [
            holder_of(block_map[own_side, own_seq, NEIGH * u + n], arrived_ref.shape[0])
            for n in range(NEIGH)
        ]
        for u in range(groups)
    ]
    firsts = jnp.concatenate([level_of(pair[0]) for pair in slots], 0)
    seconds = jnp.concatenate([level_of(pair[1]) for pair in slots], 0)
    top = jnp.maximum(firsts, seconds)
    raised = jnp.exp2(firsts - top)
    share = raised / (raised + jnp.exp2(seconds - top))
    columns = share.T
    head = last_row_mask(rows, HD)
    before = [jnp.zeros((rows, HD), jnp.float32)] * heads
    step = groups // 2
    stores = []
    for u in range(groups):
        for g in range(heads):
            cols = slice(g * HD, (g + 1) * HD)
            own = slice(g * rows, (g + 1) * rows)
            one = arrived_ref[slots[u][0], own, :].astype(jnp.float32)
            two = arrived_ref[slots[u][1], own, :].astype(jnp.float32)
            now = two + columns[own, u : u + 1] * (one - two)
            cross = jnp.where(head, before[g], now)
            out_ref[u, :, cols] = (self_ref[u, :, cols] + cross).astype(jnp.bfloat16)
            before = before[:g] + [now] + before[g + 1 :]
        if (u + 1) % step == 0:
            span = pl.ds(u + 1 - step, step)
            store = pltpu.make_async_copy(out_ref.at[span], out_hbm.at[span], sems.at[u // step])
            store.start()
            stores.append(store)
    for store in stores:
        store.wait()


def mix(place, block_map, arrived, self_out):
    groups, rows, feats = self_out.shape
    return pl.pallas_call(
        mix_kernel,
        out_shape=jax.ShapeDtypeStruct(self_out.shape, jnp.bfloat16),
        in_specs=[pl.BlockSpec(memory_space=pltpu.SMEM)] * 2 + [IN_VMEM] * 2,
        out_specs=ANYWHERE,
        scratch_shapes=[
            pltpu.VMEM(self_out.shape, jnp.bfloat16),
            pltpu.SemaphoreType.DMA((2,)),
        ],
        compiler_params=params(),
        cost_estimate=pl.CostEstimate(
            flops=8 * groups * rows * feats,
            bytes_accessed=10 * groups * rows * feats,
            transcendentals=0,
        ),
        name="mix",
    )(place, block_map, arrived, self_out)


def ring_gather(low, high, axis, asked, wanted):
    count = lax.axis_size(axis)
    up = [(i, (i + 1) % count) for i in range(count)]
    down = [(i, (i - 1) % count) for i in range(count)]
    shards = [low, high]
    right_low = left_low = low
    right_high = left_high = high
    for _ in range(1, count // 2):
        right_low = lax.ppermute(right_low, axis, up)
        left_low = lax.ppermute(left_low, axis, down)
        right_high = lax.ppermute(right_high, axis, up)
        left_high = lax.ppermute(left_high, axis, down)
        shards += [right_low, right_high, left_low, left_high]
    right_low, asked, wanted = lax.optimization_barrier((right_low, asked, wanted))
    shards.append(lax.ppermute(right_low, axis, up))
    shards.append(lax.ppermute(left_high, axis, down))
    return shards, asked, wanted


def ring_owners(axis):
    count = lax.axis_size(axis)
    here = lax.axis_index(axis)
    owners = [here]
    for hop in range(1, count // 2):
        owners += [here - hop, here + hop]
    owners.append(here + count // 2)
    return jnp.stack(owners).astype(jnp.int32) % count


def on_device(
    self_query, self_key, self_value, cross_query, passages, w_key, w_value, block_map, passage_ids
):
    side_now = lax.axis_index("side")
    seq_now = lax.axis_index("seq")
    blocks = lax.axis_size("seq")
    place = jnp.stack([side_now, seq_now]).astype(jnp.int32)
    length, feats = cross_query.shape[2:]
    groups = length // GROUP

    near = lax.ppermute(
        passages[0, 0],
        ("side", "seq"),
        [(h * blocks + b, (1 - h) * blocks + holder_of(b, blocks)) for h in range(2) for b in range(blocks)],
    )
    half = near.shape[0] // 2

    chunks = pack_queries(place, block_map, cross_query[0, 0].reshape(groups, GROUP, feats), blocks)
    asked = lax.all_to_all(chunks, "seq", split_axis=0, concat_axis=0, tiled=True)
    self_out = self_attention(self_query[0, 0], self_key[0, 0], self_value[0, 0])

    weights = order_weights(ring_owners("tp"), w_key, w_value)
    wanted = wanted_passages(place, block_map, passage_ids)
    near, weights, wanted = lax.optimization_barrier((near, weights, wanted))
    shards, asked, wanted = ring_gather(near[:half], near[half:], "tp", asked, wanted)
    answers = cross_attention(wanted, shards, weights, asked)
    arrived = lax.all_to_all(answers, "seq", split_axis=0, concat_axis=0, tiled=True)
    mixed = mix(place, block_map, arrived, self_out.reshape(groups, GROUP, feats))
    return mixed.reshape(1, 1, length, feats)


def solution(mesh):
    return jax.shard_map(
        on_device,
        mesh=mesh,
        in_specs=(
            P("side", "seq", None, "tp"),
            P("side", "seq", None, "tp"),
            P("side", "seq", None, "tp"),
            P("side", "seq", None, "tp"),
            P("side", "seq", None, None, "tp"),
            P(None, "tp"),
            P(None, "tp"),
            P(),
            P(),
        ),
        out_specs=P("side", "seq", None, "tp"),
        check_vma=False,
    )
```
